256 devices in a mesh: fsdp: 32 (over y, z), gen: 4 (over x_lo, core), tp: 2 (over x_hi).
Axes of the slice: x: 4 (x_hi: 2, x_lo: 2; x = x_hi * 2 + x_lo), y: 4, z: 8, core: 2. Of those that a mesh axis runs over, the one named last changes fastest.
Arguments:
- master_weight: float32 [2, 5120, 1024], P(None, ('fsdp', 'gen'), 'tp'), may hold values from -0.078125 to 0.078125
- gradient: float32 [2, 5120, 1024], P(None, ('fsdp', 'gen'), 'tp'), may hold values from -6 to 6
- first_moment: float32 [2, 5120, 1024], P(None, ('fsdp', 'gen'), 'tp'), may hold values from -1.8 to 1.8
- second_moment: float32 [2, 5120, 1024], P(None, ('fsdp', 'gen'), 'tp'), may hold values from 0.1 to 4
- new_inputs: bfloat16 [4096, 4, 5120], P(('fsdp', 'gen')), may hold values from -6 to 6
- queries: bfloat16 [4096, 4, 64, 128], P(('fsdp', 'gen'), None, 'tp'), may hold values from -41 to 41
- cache_keys: bfloat16 [4096, 128, 8, 128], P(('fsdp', 'gen'), None, 'tp'), may hold values from -6 to 6
- cache_values: bfloat16 [4096, 128, 8, 128], P(('fsdp', 'gen'), None, 'tp'), may hold values from -6 to 6
- prefix_lengths: int32 [4096], P(('fsdp', 'gen')), may hold values from 2 to 128
- rollout_lengths: int32 [4096], P(('fsdp', 'gen')), may hold values from 1 to 4
- destinations: int32 [4096], P(('fsdp', 'gen')), may hold values from 0 to 31, as said below
Outputs:
- new_master: float32 [2, 5120, 1024], P(None, ('fsdp', 'gen'), 'tp')
- new_first: float32 [2, 5120, 1024], P(None, ('fsdp', 'gen'), 'tp')
- new_second: float32 [2, 5120, 1024], P(None, ('fsdp', 'gen'), 'tp')
- fresh_kv: bfloat16 [4096, 4, 2, 8, 128], P(('fsdp', 'gen'), None, None, 'tp')
- returned_rows: bfloat16 [32, 4, 32, 2, 4, 8192], P('fsdp', 'gen', None, None, None, 'tp')
The draws below stay inside these ranges and needn't reach their ends.
Inputs may be any that keep to these rules, and one draw needn't show every extreme that they name: `destinations`: within the 32 rollouts of one group, no trainer shard is named more than 2 times; in every group one shard is named exactly 2 times.
All inputs are finite; a program needn't handle non-finite values.
Results may differ from the reference program's by a relative error of at most 0.0053.
Values may be sent and summed in bfloat16 or wider, within the bound.
No kernel may reach another device: no remote copies, remote signals or barrier semaphores. Data moves between devices by JAX's collectives and lax.ppermute only.
A program may use at most 128 MiB of HBM per device.

```python
import math
import jax
import jax.numpy as jnp
from jax import lax

D = 5120
HEAD = 128
KV_HEADS = 8
Q_PER_KV = 8
ROLL_DEV = 32
CACHE = 128
STEPS = 4
Q_HEADS = 64
KV_WIDTH = 1024
Q_WIDTH = 8192
ROLLOUTS = 4096
MOST = 2
N_FSDP = 32
N_GEN = 4


def draw_cache_keys(key, part):
    key = jax.random.fold_in(key, 11)
    base_keys = jnp.clip(jax.random.normal(key, (ROLLOUTS, CACHE, KV_HEADS, HEAD), jnp.float32), -6.0, 6.0)
    return base_keys.astype(jnp.bfloat16)


def draw_queries(key, part):
    key = jax.random.fold_in(key, 13)
    base_rows = jnp.clip(jax.random.normal(key, (ROLLOUTS, STEPS, Q_HEADS, HEAD), jnp.float32), -6.0, 6.0)
    return base_rows.astype(jnp.bfloat16)


def draw_destinations(key, part):
    key = jax.random.fold_in(key, 7)
    key_busy, key_others, key_shuffle = jax.random.split(key, 3)
    groups = N_FSDP * N_GEN
    busy_gen = jax.random.randint(key_busy, (N_GEN,), 0, N_FSDP)
    busy = jnp.tile(busy_gen, N_FSDP)
    other_keys = jax.random.split(key_others, groups)
    permuted = jax.vmap(lambda single: jax.random.permutation(single, N_FSDP - 1))(other_keys)
    others = (busy[:, None] + 1 + permuted) % N_FSDP
    picks = jnp.arange(ROLL_DEV - MOST) % (N_FSDP - 1)
    remainder = others[:, picks]
    filled = jnp.concatenate([jnp.broadcast_to(busy[:, None], (groups, MOST)), remainder], axis=1)
    shuffle_keys = jax.random.split(key_shuffle, groups)
    shuffle = jax.vmap(lambda single: jax.random.permutation(single, ROLL_DEV))(shuffle_keys)
    filled = jnp.take_along_axis(filled, shuffle, axis=1)
    return filled.reshape(ROLLOUTS).astype(jnp.int32)


def touch_ends(values, stream_key, low, high):
    longest = values.shape.index(max(values.shape))
    spots = []
    for shift in (0, 1):
        where = [jax.random.randint(jax.random.fold_in(stream_key, axis), (), 0, length) for axis, length in enumerate(values.shape)]
        where[longest] = (where[longest] + shift) % values.shape[longest]
        spots.append(tuple(where))
    return values.at[spots[0]].set(low).at[spots[1]].set(high)


def steps_of(rng, extent, cuts, low, top_value):
    loudness, own = 1.0, jax.random.fold_in(rng, 6)
    for axis_at, blocks in cuts:
        draws = jnp.exp(jax.random.uniform(jax.random.fold_in(own, axis_at), (blocks,), jnp.float32, low / len(cuts), top_value / len(cuts)))
        loudness = loudness * jnp.repeat(draws, extent[axis_at] // blocks).reshape([-1 if axis == axis_at else 1 for axis in range(len(extent))])
    return loudness


def scatter_about(stream_key, shape, spread, limit, cuts=(), held_as=jnp.bfloat16):
    gain = steps_of(stream_key, shape, cuts, -0.22, 0.18) if cuts else 1.0
    values = jax.random.normal(stream_key, shape, jnp.float32) * spread * gain
    return jnp.minimum(jnp.maximum(values, -limit), limit).astype(held_as)


def setup_inputs(seed: int = 0) -> dict:
    key_of = jax.random.split(jax.random.key(seed), 12)
    master_weight = scatter_about(key_of[0], (2, D, KV_WIDTH), D ** -0.5, 0.078125, ((1, 128), (2, 2)), jnp.float32)
    gradient = scatter_about(key_of[1], (2, D, KV_WIDTH), 1.0, 6.0, ((1, 128), (2, 2)), jnp.float32)
    first_moment = scatter_about(key_of[2], (2, D, KV_WIDTH), 0.3, 1.8, ((1, 128), (2, 2)), jnp.float32)
    second_moment = jnp.clip(jnp.exp(math.log(4.0) - 3.6888794 * jax.random.uniform(key_of[3], (2, D, KV_WIDTH), jnp.float32) ** steps_of(key_of[3], (2, D, KV_WIDTH), ((1, 128), (2, 2)), -0.2, 0.2)), 0.1, 4.0)
    new_inputs = scatter_about(key_of[4], (ROLLOUTS, STEPS, D), 1.0, 6.0, ((0, 128),))
    queries = draw_queries(jax.random.fold_in(key_of[11], 71), 0)
    cache_keys = draw_cache_keys(jax.random.fold_in(key_of[11], 71), 0)
    cache_values = scatter_about(key_of[7], (ROLLOUTS, CACHE, KV_HEADS, HEAD), 1.0, 6.0, ((0, 128), (2, 2)))
    prefix_lengths = touch_ends(jax.random.randint(key_of[8], (ROLLOUTS,), 2, CACHE + 1), jax.random.fold_in(key_of[8], 1), 2, CACHE).astype(jnp.int32)
    rollout_lengths = touch_ends(jax.random.randint(key_of[9], (ROLLOUTS,), 1, STEPS + 1), jax.random.fold_in(key_of[9], 1), 1, STEPS).astype(jnp.int32)
    destinations = draw_destinations(jax.random.fold_in(key_of[11], 71), 0)
    return dict(master_weight=master_weight, gradient=gradient, first_moment=first_moment, second_moment=second_moment, new_inputs=new_inputs, queries=queries, cache_keys=cache_keys, cache_values=cache_values, prefix_lengths=prefix_lengths, rollout_lengths=rollout_lengths, destinations=destinations)


beta_one = 0.9
beta_two = 0.95
adam_eps = 1e-08
learn_rate = 0.002
weight_decay = 0.1
adam_step = 10.0
rope_theta = 1000000.0
norm_eps = 1e-06
masked_score = -1e+30

def adam_update(master_weight, gradient, first_moment, second_moment):
    first_next = beta_one * first_moment + (1.0 - beta_one) * gradient
    second_next = beta_two * second_moment + (1.0 - beta_two) * gradient * gradient
    first_hat = first_next / (1.0 - beta_one ** adam_step)
    second_hat = second_next / (1.0 - beta_two ** adam_step)
    master_next = master_weight - learn_rate * (first_hat / (jnp.sqrt(second_hat) + adam_eps) + weight_decay * master_weight)
    return (master_next, first_next, second_next)

def rotate(vectors, positions):
    half_size = vectors.shape[-1] // 2
    exponent = -2.0 * jnp.arange(half_size).astype(jnp.float32) / vectors.shape[-1]
    inverse_freq = jnp.power(jnp.float32(rope_theta), exponent)
    angle = positions.astype(jnp.float32)[..., None] * inverse_freq
    cosine = jnp.cos(angle)
    sine = jnp.sin(angle)
    first_half = vectors[..., :half_size]
    second_half = vectors[..., half_size:]
    return jnp.concatenate([first_half * cosine - second_half * sine, second_half * cosine + first_half * sine], axis=-1)

def key_norm(raw_keys):
    return raw_keys / jnp.sqrt(lax.optimization_barrier(jnp.mean(raw_keys * raw_keys, axis=-1, keepdims=True)) + norm_eps)

def attend_one(operands):
    query_rows, keys_old, values_old, keys_new, values_new, prefix = operands
    score_scale = HEAD ** (-0.5)
    grouped = query_rows.reshape(STEPS, KV_HEADS, Q_PER_KV, HEAD).astype(jnp.float32)
    old_scores = jnp.einsum('sgqh,cgh->gqsc', grouped, keys_old.astype(jnp.float32)) * score_scale
    new_scores = jnp.einsum('sgqh,tgh->gqst', grouped, keys_new.astype(jnp.float32)) * score_scale
    old_mask = jnp.arange(CACHE) < prefix
    new_mask = jnp.arange(STEPS)[None, :] <= jnp.arange(STEPS)[:, None]
    old_scores = jnp.where(old_mask, old_scores, masked_score)
    new_scores = jnp.where(new_mask, new_scores, masked_score)
    row_max = jnp.maximum(lax.optimization_barrier(jnp.max(old_scores, axis=-1)), lax.optimization_barrier(jnp.max(new_scores, axis=-1)))
    old_exp = jnp.exp(old_scores - row_max[..., None])
    new_exp = jnp.exp(new_scores - row_max[..., None])
    row_total = lax.optimization_barrier(jnp.sum(old_exp, axis=-1)) + lax.optimization_barrier(jnp.sum(new_exp, axis=-1))
    old_weight = (old_exp / row_total[..., None]).astype(jnp.bfloat16)
    new_weight = (new_exp / row_total[..., None]).astype(jnp.bfloat16)
    mixed = jnp.einsum('gqsc,cgh->sgqh', old_weight.astype(jnp.float32), values_old.astype(jnp.float32))
    mixed = mixed + jnp.einsum('gqst,tgh->sgqh', new_weight.astype(jnp.float32), values_new.astype(jnp.float32))
    return mixed.astype(jnp.bfloat16).reshape(STEPS, Q_WIDTH)

def reference(master_weight, gradient, first_moment, second_moment, new_inputs, queries, cache_keys, cache_values, prefix_lengths, rollout_lengths, destinations):
    new_master, new_first, new_second = adam_update(master_weight, gradient, first_moment, second_moment)
    weight_bf = new_master.astype(jnp.bfloat16)
    flat_inputs = new_inputs.reshape(ROLLOUTS * STEPS, D)
    raw_keys = jnp.dot(flat_inputs, weight_bf[0], preferred_element_type=jnp.float32)
    raw_values = jnp.dot(flat_inputs, weight_bf[1], preferred_element_type=jnp.float32)
    raw_keys = raw_keys.reshape(ROLLOUTS, STEPS, KV_HEADS, HEAD)
    raw_values = raw_values.reshape(ROLLOUTS, STEPS, KV_HEADS, HEAD)
    positions = (prefix_lengths[:, None] + jnp.arange(STEPS, dtype=jnp.int32)[None, :]).astype(jnp.int32)
    fresh_keys = rotate(key_norm(raw_keys), positions[:, :, None]).astype(jnp.bfloat16)
    fresh_values = raw_values.astype(jnp.bfloat16)
    fresh_kv = jnp.stack([fresh_keys, fresh_values], axis=2)
    attention = lax.map(attend_one, (queries, cache_keys, cache_values, fresh_keys, fresh_values, prefix_lengths))
    kept = jnp.arange(STEPS)[None, :] < rollout_lengths[:, None]
    token_rows = jnp.where(kept[:, :, None], attention, jnp.zeros_like(attention))
    block_dest = destinations.reshape(N_FSDP * N_GEN, ROLL_DEV)
    same_dest = block_dest[:, :, None] == block_dest[:, None, :]
    earlier = jnp.arange(ROLL_DEV)[None, :] < jnp.arange(ROLL_DEV)[:, None]
    slot_rank = lax.optimization_barrier(jnp.sum((same_dest & earlier[None]).astype(jnp.int32), axis=2)).reshape(ROLLOUTS).astype(jnp.int32)
    block_index = (jnp.arange(ROLLOUTS) // ROLL_DEV).astype(jnp.int32)
    fsdp_index = (block_index // N_GEN).astype(jnp.int32)
    gen_index = (block_index % N_GEN).astype(jnp.int32)
    returned_rows = jnp.zeros((N_FSDP, N_GEN, N_FSDP, MOST, STEPS, Q_WIDTH), jnp.bfloat16)
    returned_rows = returned_rows.at[destinations, gen_index, fsdp_index, slot_rank].set(token_rows)
    return (new_master, new_first, new_second, fresh_kv, returned_rows)
```

```python
import functools
import jax
import jax.numpy as jnp
from jax import lax
from jax.experimental import pallas as pl
from jax.experimental.pallas import tpu as pltpu
from jax.sharding import Mesh, PartitionSpec as P

beta_one = 0.9
beta_two = 0.95
adam_eps = 1e-08
learn_rate = 0.002
weight_decay = 0.1
adam_step = 10.0
rope_theta = 1000000.0
norm_eps = 1e-06
masked_score = -1e30

N_Y = 4
N_Z = 8
N_GEN = 4
N_FSDP = N_Y * N_Z
HEAD = 128
HEADS = 4
STEPS = 4
ROLL = 32
TOKENS = ROLL * STEPS
CACHE = 128
ROWS = 40
DEPTH = 1280
SLOTS = 2
SCALE = HEAD ** (-0.5)
F32 = jnp.float32
BF16 = jnp.bfloat16
VMEM_BYTES = 48 * 1024 * 1024


def params(**more):
    return pltpu.CompilerParams(vmem_limit_bytes=VMEM_BYTES, **more)


def whole():
    return pl.BlockSpec(memory_space=pltpu.VMEM)


def iota(shape, axis):
    return lax.broadcasted_iota(jnp.int32, shape, axis)


def adam_kernel(master_ref, grad_ref, first_ref, second_ref, m_out, f_out, s_out, w_out):
    for kv in range(2):
        grad = grad_ref[kv]
        master = master_ref[kv]
        first = beta_one * first_ref[kv] + (1.0 - beta_one) * grad
        second = beta_two * second_ref[kv] + (1.0 - beta_two) * grad * grad
        first_hat = first / (1.0 - beta_one**adam_step)
        second_hat = second / (1.0 - beta_two**adam_step)
        master = master - learn_rate * (
            first_hat / (jnp.sqrt(second_hat) + adam_eps) + weight_decay * master
        )
        f_out[kv] = first
        s_out[kv] = second
        m_out[kv] = master
        rounded = master.astype(BF16)
        for q in range(N_GEN):
            piece = rounded[:, q * HEAD : (q + 1) * HEAD]
            for z in range(N_Z):
                w_out[z, q, :, kv * HEAD : (kv + 1) * HEAD] = piece


def adam(master, grad, first, second):
    shape = jax.ShapeDtypeStruct(master.shape, F32)
    return pl.pallas_call(
        adam_kernel,
        out_shape=(shape, shape, shape, jax.ShapeDtypeStruct((N_Z, N_GEN, ROWS, 2 * HEAD), BF16)),
        in_specs=[whole()] * 4,
        out_specs=(whole(),) * 4,
        compiler_params=params(),
        name="adam",
    )(master, grad, first, second)


OLD_BLOCK = 4


def old_kernel(prefix, dest, slot, q_ref, k_ref, v_ref, out_ref, lse_ref, qp_ref, ok_ref):
    step = pl.program_id(0)
    span = CACHE * HEADS

    @pl.when(step == 0)
    def _():
        out_ref[...] = jnp.zeros_like(out_ref)
        row, col = iota((TOKENS, span), 0), iota((TOKENS, span), 1)
        ok_ref[...] = jnp.where(col % HEADS == row // 32, col, CACHE * HEADS)

    row, col = iota((TOKENS, TOKENS), 0), iota((TOKENS, TOKENS), 1)
    perm = ((col % 32 == row // 4) & (col // 32 == row % 4)).astype(BF16)
    eye = row == col
    place = ok_ref[...]
    lses = []
    for n in range(OLD_BLOCK):
        r = step * OLD_BLOCK + n
        query = jnp.dot(perm, q_ref[n], preferred_element_type=F32).astype(BF16)
        qp_ref[n] = query
        score = lax.dot_general(
            query, k_ref[n], (((1,), (1,)), ((), ())), preferred_element_type=F32
        )
        score = jnp.where(place < prefix[r] * HEADS, score * SCALE, masked_score)
        top = jnp.max(score, axis=1, keepdims=True)
        weight = jnp.exp(score - top)
        total = jnp.sum(weight, axis=1, keepdims=True)
        mixed = jnp.dot(weight.astype(BF16), v_ref[n], preferred_element_type=F32)
        out_ref[dest[r], slot[r]] = (mixed / total).astype(BF16)
        lse = top + jnp.log(total)
        lses.append(jnp.sum(jnp.where(eye, lse, 0.0), axis=0, keepdims=True))
    for n in range(0, OLD_BLOCK, 2):
        lse_ref[pl.ds((step * OLD_BLOCK + n) // 2, 1), :] = jnp.concatenate(
            [lses[n], lses[n + 1]], axis=1
        )


def old_attention(prefix, dest, slot, queries, keys, values):
    span = CACHE * HEADS
    return pl.pallas_call(
        old_kernel,
        grid_spec=pltpu.PrefetchScalarGridSpec(
            num_scalar_prefetch=3,
            grid=(ROLL // OLD_BLOCK,),
            in_specs=[
                pl.BlockSpec((OLD_BLOCK, TOKENS, HEAD), lambda i, *_: (i, 0, 0)),
                pl.BlockSpec((OLD_BLOCK, span, HEAD), lambda i, *_: (i, 0, 0)),
                pl.BlockSpec((OLD_BLOCK, span, HEAD), lambda i, *_: (i, 0, 0)),
            ],
            out_specs=(
                pl.BlockSpec((N_FSDP, SLOTS, TOKENS, HEAD), lambda i, *_: (0, 0, 0, 0)),
                pl.BlockSpec((ROLL // 2, 2 * TOKENS), lambda i, *_: (0, 0)),
                pl.BlockSpec((OLD_BLOCK, TOKENS, HEAD), lambda i, *_: (i, 0, 0)),
            ),
            scratch_shapes=[pltpu.VMEM((TOKENS, span), jnp.int32)],
        ),
        out_shape=(
            jax.ShapeDtypeStruct((N_FSDP, SLOTS, TOKENS, HEAD), BF16),
            jax.ShapeDtypeStruct((ROLL // 2, 2 * TOKENS), F32),
            jax.ShapeDtypeStruct((ROLL, TOKENS, HEAD), BF16),
        ),
        compiler_params=params(),
        cost_estimate=pl.CostEstimate(
            flops=2 * 2 * ROLL * TOKENS * span * HEAD,
            bytes_accessed=13 * 1024 * 1024,
            transcendentals=ROLL * TOKENS * span,
        ),
        name="old_attention",
    )(prefix, dest, slot, queries, keys, values)


def project_kernel(me, w_ref, x0, x1, x2, x3, out_ref):
    weight = w_ref[...]
    for j, x in enumerate((x0, x1, x2, x3)):
        out_ref[0, me[0] ^ j] = jnp.dot(
            x[0], weight, preferred_element_type=F32
        ).astype(BF16)


def project(me, weight, pieces):
    return pl.pallas_call(
        project_kernel,
        grid_spec=pltpu.PrefetchScalarGridSpec(
            num_scalar_prefetch=1,
            grid=(N_Y,),
            in_specs=[pl.BlockSpec((DEPTH, 2 * HEAD), lambda i, *_: (0, 0))]
            + [pl.BlockSpec((1, TOKENS, DEPTH), lambda i, *_: (i, 0, 0))] * 4,
            out_specs=pl.BlockSpec((1, N_GEN, TOKENS, 2 * HEAD), lambda i, *_: (i, 0, 0, 0)),
        ),
        out_shape=jax.ShapeDtypeStruct((N_Y, N_GEN, TOKENS, 2 * HEAD), BF16),
        compiler_params=params(),
        cost_estimate=pl.CostEstimate(
            flops=2 * N_Y * N_GEN * TOKENS * DEPTH * 2 * HEAD,
            bytes_accessed=7 * 1024 * 1024,
            transcendentals=0,
        ),
        name="project",
    )(me, weight, *pieces)


def fresh_kernel(
    dest, slot, lengths, part_ref, cos_ref, sin_ref, qp_ref, lse_ref, kv_ref, late_ref, kf, vf, wf
):
    cosine, sine = cos_ref[...], sin_ref[...]
    for g in range(HEADS):
        total = part_ref[0, g].astype(F32)
        for y in range(1, N_Y):
            total = total + part_ref[y, g].astype(F32)
        key, value = total[:, :HEAD], total[:, HEAD:]
        key = key / jnp.sqrt(jnp.mean(key * key, axis=-1, keepdims=True) + norm_eps)
        key = key * cosine + pltpu.roll(key, HEAD // 2, 1) * sine
        key, value = key.astype(BF16), value.astype(BF16)
        kv_ref[0, g] = key
        kv_ref[1, g] = value
        kf[g] = key.astype(F32)
        vf[g] = value.astype(F32)
    late_ref[...] = jnp.zeros_like(late_ref)
    wf[...] = jnp.zeros_like(wf)

    row, col = iota((32, 256), 0), iota((32, 256), 1)
    own = (
        (row // 8 == (col % 128) // 32)
        & ((row % 8) // 4 == col // 128)
        & (row % 4 <= col % 4)
    )
    lane = iota((1, 256), 1)
    row8 = iota((8, 128), 0)

    def pair(p, carry):
        keys = jnp.concatenate(
            [kf[g, pl.ds(pl.multiple_of(p * 8, 8), 8), :] for g in range(HEADS)], axis=0
        ).astype(BF16)
        query = qp_ref[pl.ds(2 * p, 2)].reshape(2 * TOKENS, HEAD)
        score = lax.dot_general(
            keys, query, (((1,), (1,)), ((), ())), preferred_element_type=F32
        )
        score = jnp.where(own, score * SCALE, masked_score)
        old = lse_ref[pl.ds(p, 1), :]
        top = jnp.maximum(jnp.max(score, axis=0, keepdims=True), old)
        weight = jnp.exp(score - top)
        alpha = jnp.exp(old - top)
        total = jnp.sum(weight, axis=0, keepdims=True) + alpha
        kept = (lane % STEPS) < jnp.where(lane < 128, lengths[2 * p], lengths[2 * p + 1])
        scale = jnp.where(kept, 1.0 / total, 0.0)
        weight = weight * scale
        alpha = alpha * scale
        weight = weight[0:8] + weight[8:16] + weight[16:24] + weight[24:32]
        vals = [vf[g, pl.ds(pl.multiple_of(p * 8, 8), 8), :] for g in range(HEADS)]
        for rr in range(2):
            r = 2 * p + rr
            d, j = dest[r], slot[r]
            mine = weight[:, rr * 128 : (rr + 1) * 128]
            if rr:
                mine = pltpu.roll(mine, 4, 0)
            mine = jnp.where(row8 == 4, alpha[:, rr * 128 : (rr + 1) * 128], mine)
            wf[d, pl.ds(pl.multiple_of(j * 8, 8), 8), :] = mine
            tiles = []
            for g in range(0, HEADS, 2):
                first, second = vals[g], vals[g + 1]
                if rr:
                    first = pltpu.roll(first, 4, 0)
                else:
                    second = pltpu.roll(second, 4, 0)
                tiles.append(jnp.where(row8 < 4, first, second))
            late_ref[d, pl.ds(pl.multiple_of(j * 16, 16), 16), :] = jnp.concatenate(
                tiles, axis=0
            ).astype(BF16)
        return carry

    lax.fori_loop(0, ROLL // 2, pair, 0, unroll=4)
    late_ref[:, 32:48, :] = wf[...].astype(BF16)


def fresh(dest, slot, lengths, parts, cosine, sine, queries, lse):
    smem = pl.BlockSpec(memory_space=pltpu.SMEM)
    return pl.pallas_call(
        fresh_kernel,
        in_specs=[smem] * 3 + [whole()] * 5,
        out_specs=(whole(), whole()),
        out_shape=(
            jax.ShapeDtypeStruct((2, HEADS, TOKENS, HEAD), BF16),
            jax.ShapeDtypeStruct((N_FSDP, 48, HEAD), BF16),
        ),
        scratch_shapes=[
            pltpu.VMEM((HEADS, TOKENS, HEAD), F32),
            pltpu.VMEM((HEADS, TOKENS, HEAD), F32),
            pltpu.VMEM((N_FSDP, 16, HEAD), F32),
        ],
        compiler_params=params(),
        cost_estimate=pl.CostEstimate(
            flops=2 * 32 * 32 * 256 * 128, bytes_accessed=3 * 1024 * 1024, transcendentals=1000000
        ),
        name="fresh",
    )(dest, slot, lengths, parts, cosine, sine, queries, lse)


JOIN_BLOCK = 8


def join_kernel(old_ref, late_ref, out_ref):
    row, col = iota((TOKENS, TOKENS), 0), iota((TOKENS, TOKENS), 1)
    eye = row == col
    row8 = iota((8, 128), 0)
    row16, lane = iota((16, 128), 0), iota((16, 128), 1)
    same = lane // 32 == row16 // 4
    for n in range(JOIN_BLOCK):
        tile = late_ref[n, 32:48, :].astype(F32)
        for j in range(SLOTS):
            mine = tile[j * 8 : (j + 1) * 8]
            alpha = mine[4:5]
            diag = jnp.where(eye, alpha, 0.0).astype(BF16)
            mixed = jnp.dot(diag, old_ref[n, j], preferred_element_type=F32)
            both = jnp.where(row8 < 4, mine, pltpu.roll(mine, 4, 0))
            weight = jnp.where(same, jnp.concatenate([both, both], axis=0), 0.0).astype(BF16)
            value = late_ref[n, j * 16 : (j + 1) * 16, :]
            mixed = mixed + lax.dot_general(
                weight, value, (((0,), (0,)), ((), ())), preferred_element_type=F32
            )
            out_ref[n, j] = mixed.astype(BF16)


def join(old, late):
    return pl.pallas_call(
        join_kernel,
        grid=(N_FSDP // JOIN_BLOCK,),
        in_specs=[
            pl.BlockSpec((JOIN_BLOCK, SLOTS, TOKENS, HEAD), lambda i: (i, 0, 0, 0)),
            pl.BlockSpec((JOIN_BLOCK, 48, HEAD), lambda i: (i, 0, 0)),
        ],
        out_specs=pl.BlockSpec((JOIN_BLOCK, SLOTS, TOKENS, HEAD), lambda i: (i, 0, 0, 0)),
        out_shape=jax.ShapeDtypeStruct((N_FSDP, SLOTS, TOKENS, HEAD), BF16),
        compiler_params=params(),
        cost_estimate=pl.CostEstimate(
            flops=2 * 64 * 144 * 128 * 128, bytes_accessed=5 * 1024 * 1024, transcendentals=0
        ),
        name="join",
    )(old, late)


def turn_tables(prefix_lengths):
    half_size = HEAD // 2
    exponent = -2.0 * jnp.arange(half_size).astype(F32) / HEAD
    inverse_freq = jnp.power(jnp.float32(rope_theta), exponent)
    positions = prefix_lengths[:, None] + jnp.arange(STEPS, dtype=jnp.int32)[None, :]
    angle = positions.reshape(TOKENS, 1).astype(F32) * inverse_freq
    cosine, sine = jnp.cos(angle), jnp.sin(angle)
    return (
        jnp.concatenate([cosine, cosine], axis=-1),
        jnp.concatenate([-sine, sine], axis=-1),
    )


def at(x):
    return (x % 2) * 2 + x // 2


def on_device(
    master_weight,
    gradient,
    first_moment,
    second_moment,
    new_inputs,
    queries,
    cache_keys,
    cache_values,
    prefix_lengths,
    rollout_lengths,
    destinations,
):
    new_master, new_first, new_second, blocks = adam(
        master_weight, gradient, first_moment, second_moment
    )
    weight = lax.all_to_all(
        blocks.reshape(N_Z * N_GEN, ROWS, 2 * HEAD), ("z", "xl", "c"), 0, 0, tiled=True
    ).reshape(DEPTH, 2 * HEAD)

    columns = new_inputs.reshape(TOKENS, N_Y, DEPTH).transpose(1, 0, 2)
    own = lax.all_to_all(columns, "y", 0, 0, tiled=True)
    ring = [(at(x), at((x + 1) % 4)) for x in range(4)]
    back = [(at(x), at((x + 3) % 4)) for x in range(4)]
    swap = [(0, 1), (1, 0)]
    far = jnp.concatenate(
        [
            lax.ppermute(own[: N_Y // 2], ("xl", "tp"), ring),
            lax.ppermute(own[N_Y // 2 :], ("xl", "tp"), back),
        ],
        axis=0,
    )
    near = lax.ppermute(own, "c", swap)
    both = lax.ppermute(far, "c", swap)

    same_dest = destinations[:, None] == destinations[None, :]
    earlier = jnp.arange(ROLL)[None, :] < jnp.arange(ROLL)[:, None]
    slot_rank = jnp.sum((same_dest & earlier).astype(jnp.int32), axis=1)
    old_rows, lse, ordered = old_attention(
        prefix_lengths,
        destinations,
        slot_rank,
        queries.reshape(ROLL, TOKENS, HEAD),
        cache_keys.reshape(ROLL, CACHE * HEADS, HEAD),
        cache_values.reshape(ROLL, CACHE * HEADS, HEAD),
    )
    old_in = lax.all_to_all(old_rows, ("y", "z"), 0, 0, tiled=True)

    me = (lax.axis_index("xl") * 2 + lax.axis_index("c")).reshape(1)
    parts = project(me, weight, (own, near, far, both))
    parts = lax.all_to_all(
        parts.reshape(N_Y * N_GEN, TOKENS, 2 * HEAD), ("y", "xl", "c"), 0, 0, tiled=True
    ).reshape(N_Y, N_GEN, TOKENS, 2 * HEAD)
    cosine, sine = turn_tables(prefix_lengths)
    fresh_parts, late = fresh(
        destinations, slot_rank, rollout_lengths, parts, cosine, sine, ordered, lse
    )
    late_in = lax.all_to_all(late, ("y", "z"), 0, 0, tiled=True)
    fresh_kv = fresh_parts.reshape(2, HEADS, ROLL, STEPS, HEAD).transpose(2, 3, 0, 1, 4)
    joined = join(old_in, late_in)
    returned = joined.reshape(N_FSDP, SLOTS, 8 * HEADS, STEPS, HEAD).transpose(0, 1, 3, 2, 4)
    returned_rows = returned.reshape(1, 1, N_FSDP, SLOTS, STEPS, 8 * HEADS * HEAD)
    return (new_master, new_first, new_second, fresh_kv, returned_rows)


def solution(mesh):
    fine = Mesh(mesh.devices.reshape(N_Y, N_Z, 2, 2, 2), ("y", "z", "xl", "c", "tp"))
    group = ("y", "z", "xl", "c")
    rows = P(None, group, "tp")
    in_specs = (
        rows,
        rows,
        rows,
        rows,
        P(group, None, None),
        P(group, None, "tp", None),
        P(group, None, "tp", None),
        P(group, None, "tp", None),
        P(group),
        P(group),
        P(group),
    )
    out_specs = (
        rows,
        rows,
        rows,
        P(group, None, None, "tp", None),
        P(("y", "z"), ("xl", "c"), None, None, None, "tp"),
    )
    return jax.shard_map(
        on_device, mesh=fine, in_specs=in_specs, out_specs=out_specs, check_vma=False
    )
```

```python
import functools
import jax
import jax.numpy as jnp
from jax import lax
from jax.experimental import pallas as pl
from jax.experimental.pallas import tpu as pltpu
from jax.sharding import Mesh, PartitionSpec as P

beta_one = 0.9
beta_two = 0.95
adam_eps = 1e-08
learn_rate = 0.002
weight_decay = 0.1
adam_step = 10.0
rope_theta = 1000000.0
norm_eps = 1e-06
masked_score = -1e30

N_Y = 4
N_Z = 8
N_GEN = 4
N_FSDP = N_Y * N_Z
HEAD = 128
HEADS = 4
STEPS = 4
ROLL = 32
TOKENS = ROLL * STEPS
CACHE = 128
ROWS = 40
DEPTH = 1280
SLOTS = 2
SCALE = HEAD ** (-0.5)
F32 = jnp.float32
BF16 = jnp.bfloat16
VMEM_BYTES = 40 * 1024 * 1024
VMEM_MOST = 60 * 1024 * 1024


SMALL = pl.CostEstimate(flops=1000, bytes_accessed=1000, transcendentals=0)


def params(limit=VMEM_BYTES):
    return pltpu.CompilerParams(vmem_limit_bytes=limit)


def whole():
    return pl.BlockSpec(memory_space=pltpu.VMEM)


def iota(shape, axis):
    return lax.broadcasted_iota(jnp.int32, shape, axis)


def after(value, *others):
    anywhere = pl.BlockSpec(memory_space=pl.ANY)
    return pl.pallas_call(
        lambda *refs: None,
        in_specs=[anywhere] * (1 + len(others)),
        out_specs=anywhere,
        out_shape=jax.ShapeDtypeStruct(value.shape, value.dtype),
        input_output_aliases={0: 0},
        cost_estimate=SMALL,
        name="after",
    )(value, *others)


def adam_kernel(*refs):
    sources, (m_out, f_out, s_out, w_out) = refs[:4], refs[4:8]
    held, sems = refs[8], refs[9]
    copies = [
        pltpu.make_async_copy(source, held.at[i], sems.at[i]) for i, source in enumerate(sources)
    ]
    for copy in copies:
        copy.start()
    for copy in copies:
        copy.wait()
    for kv in range(2):
        master, grad, first, second = (held[i, kv] for i in range(4))
        first = beta_one * first + (1.0 - beta_one) * grad
        second = beta_two * second + (1.0 - beta_two) * grad * grad
        first_hat = first / (1.0 - beta_one**adam_step)
        second_hat = second / (1.0 - beta_two**adam_step)
        master = master - learn_rate * (
            first_hat / (jnp.sqrt(second_hat) + adam_eps) + weight_decay * master
        )
        f_out[kv] = first
        s_out[kv] = second
        m_out[kv] = master
        rounded = master.astype(BF16)
        for q in range(N_GEN):
            piece = rounded[:, q * HEAD : (q + 1) * HEAD]
            for z in range(N_Z):
                w_out[z, q, :, kv * HEAD : (kv + 1) * HEAD] = piece


def adam(master, grad, first, second):
    shape = jax.ShapeDtypeStruct(master.shape, F32)
    return pl.pallas_call(
        adam_kernel,
        out_shape=(shape, shape, shape, jax.ShapeDtypeStruct((N_Z, N_GEN, ROWS, 2 * HEAD), BF16)),
        in_specs=[pl.BlockSpec(memory_space=pl.ANY)] * 4,
        out_specs=(whole(),) * 4,
        scratch_shapes=[
            pltpu.VMEM((4,) + master.shape, F32),
            pltpu.SemaphoreType.DMA((4,)),
        ],
        compiler_params=params(VMEM_MOST),
        cost_estimate=SMALL,
        name="adam",
    )(master, grad, first, second)


def columns_kernel(x_ref, _, out_ref, low_ref, high_ref):
    block = x_ref[...].reshape(TOKENS, DEPTH)
    out_ref[0] = block
    low_ref[0] = block[: TOKENS // 2]
    high_ref[0] = block[TOKENS // 2 :]


def columns(inputs, later):
    def shape(rows):
        return jax.ShapeDtypeStruct((N_Y, rows, DEPTH), BF16)

    def block(rows):
        return pl.BlockSpec((1, rows, DEPTH), lambda i: (i, 0, 0))

    return pl.pallas_call(
        columns_kernel,
        grid=(N_Y,),
        in_specs=[
            pl.BlockSpec((ROLL, STEPS, DEPTH), lambda i: (0, 0, i)),
            pl.BlockSpec(memory_space=pl.ANY),
        ],
        out_specs=(block(TOKENS), block(TOKENS // 2), block(TOKENS // 2)),
        out_shape=(shape(TOKENS), shape(TOKENS // 2), shape(TOKENS // 2)),
        compiler_params=params(),
        cost_estimate=SMALL,
        name="columns",
    )(inputs, later)


OLD_BLOCK = 8
PIECE = TOKENS // N_Y
LOG2E = 1.4426950408889634


def old_kernel(prefix, q_ref, k_ref, v_ref, _, out_ref, lse_ref, qp_ref, bias_ref):
    step = pl.program_id(0)
    span = CACHE * HEADS
    block = range(OLD_BLOCK)

    @pl.when(step == 0)
    def _():
        row, col = iota((TOKENS, span), 0), iota((TOKENS, span), 1)
        bias_ref[...] = jnp.where(col % HEADS == row // 32, 0.0, masked_score)

    row, col = iota((TOKENS, TOKENS), 0), iota((TOKENS, TOKENS), 1)
    perm = ((col % 32 == row // 4) & (col // 32 == row % 4)).astype(BF16)
    lane = iota((1, span), 1)
    query = [
        jnp.dot(perm, q_ref[n], preferred_element_type=F32).astype(BF16) for n in block
    ]
    for n in block:
        qp_ref[n] = query[n]
    score = [
        lax.dot_general(
            query[n], k_ref[n], (((1,), (1,)), ((), ())), preferred_element_type=F32
        )
        for n in block
    ]
    score = [
        score[n]
        + bias_ref[...]
        + jnp.where(lane < prefix[step * OLD_BLOCK + n] * HEADS, 0.0, masked_score)
        for n in block
    ]
    top = [jnp.max(s, axis=1, keepdims=True) for s in score]
    weight = [jnp.exp2((s - t) * (SCALE * LOG2E)) for s, t in zip(score, top)]
    total = [jnp.sum(w, axis=1, keepdims=True) for w in weight]
    mixed = [
        jnp.dot(weight[n].astype(BF16), v_ref[n], preferred_element_type=F32) for n in block
    ]
    for n in block:
        out_ref[n] = mixed[n] * (1.0 / total[n])
        lse_ref[n] = jnp.broadcast_to(top[n] * SCALE + jnp.log(total[n]), (TOKENS, HEAD))


def old_attention(prefix, queries, keys, values, later):
    span = CACHE * HEADS
    inside = pl.BlockSpec((OLD_BLOCK, TOKENS, HEAD), lambda i, *_: (i, 0, 0))
    cache = pl.BlockSpec((OLD_BLOCK, span, HEAD), lambda i, *_: (i, 0, 0))
    rows = (ROLL, TOKENS, HEAD)
    return pl.pallas_call(
        old_kernel,
        grid_spec=pltpu.PrefetchScalarGridSpec(
            num_scalar_prefetch=1,
            grid=(ROLL // OLD_BLOCK,),
            in_specs=[inside, cache, cache, pl.BlockSpec(memory_space=pl.ANY)],
            out_specs=(inside, inside, inside),
            scratch_shapes=[pltpu.VMEM((TOKENS, span), F32)],
        ),
        out_shape=(
            jax.ShapeDtypeStruct(rows, F32),
            jax.ShapeDtypeStruct(rows, F32),
            jax.ShapeDtypeStruct(rows, BF16),
        ),
        compiler_params=params(VMEM_MOST),
        cost_estimate=SMALL,
        name="old_attention",
    )(prefix, queries, keys, values, later)


def halves_kernel(before, beyond, _, low, high):
    half = DEPTH // 2
    low[...] = before[:half]
    high[...] = beyond[half:]


def halves(before, beyond, later):
    shape = jax.ShapeDtypeStruct((DEPTH // 2, 2 * HEAD), BF16)
    return pl.pallas_call(
        halves_kernel,
        in_specs=[whole(), whole(), pl.BlockSpec(memory_space=pl.ANY)],
        out_specs=(whole(),) * 2,
        out_shape=(shape,) * 2,
        compiler_params=params(),
        cost_estimate=SMALL,
        name="halves",
    )(before, beyond, later)


def project_kernel(shifts, sources, carried, last, me, *refs):
    weights, refs = refs[: len(shifts)], refs[len(shifts) :]
    own, near, *far = refs[: 2 if sources == 2 else 6]
    out_ref = refs[-1]
    half = TOKENS // 2
    places = [(own, 0, 0, TOKENS), (near, 1, 0, TOKENS)]
    for n, ref in enumerate(far):
        places.append((ref, 2 + n // 2, n % 2 * half, n % 2 * half + half))
    for ref, j, start, stop in places:
        total = refs[-2][j, start:stop] if j < carried else None
        at = 0
        for n, (shift, weight) in enumerate(zip(shifts, weights)):
            if n == 0 and j < carried and shift == 0:
                continue
            part = (me[0] + (N_Y - shift)) % N_Y
            depth = weight.shape[0]
            term = jnp.dot(ref[part, :, at : at + depth], weight[...], preferred_element_type=F32)
            total = term if total is None else total + term
            at = (at + depth) % DEPTH
        if last:
            key, value = total[:, :HEAD], total[:, HEAD:]
            high = key.astype(BF16)
            out_ref[j, start:stop, :HEAD] = high
            out_ref[j, start:stop, HEAD : 2 * HEAD] = (key - high.astype(F32)).astype(BF16)
            out_ref[j, start:stop, 2 * HEAD :] = value.astype(BF16)
        else:
            out_ref[j, start:stop] = total


def project(me, shifts, weights, inputs, total, last):
    width, dtype = (3 * HEAD, BF16) if last else (2 * HEAD, F32)
    sources = 2 if len(inputs) == 2 else N_GEN
    carried = () if total is None else (total,)
    return pl.pallas_call(
        functools.partial(
            project_kernel, shifts, sources, 0 if total is None else total.shape[0], last
        ),
        in_specs=[pl.BlockSpec(memory_space=pltpu.SMEM)]
        + [whole()] * (len(weights) + len(inputs) + len(carried)),
        out_specs=whole(),
        out_shape=jax.ShapeDtypeStruct((sources, TOKENS, width), dtype),
        compiler_params=params(),
        cost_estimate=SMALL,
        name="project",
    )(me, *weights, *inputs, *carried)


FRESH_BLOCK = 16
QUAD = 4


def fresh_kernel(
    dest, slot, lengths, me, p0, p1, p2, p3, cos_ref, sin_ref, qp_ref, lse_ref, old_ref,
    kv_ref, out_ref,
):
    step = pl.program_id(0)

    @pl.when(step == 0)
    def _():
        cosine, sine = cos_ref[...], sin_ref[...]
        for j, part in enumerate((p0, p1, p2, p3)):
            g = me[1] ^ j
            key = part[:, :HEAD].astype(F32) + part[:, HEAD : 2 * HEAD].astype(F32)
            key = key / jnp.sqrt(jnp.mean(key * key, axis=-1, keepdims=True) + norm_eps)
            key = key * cosine + pltpu.roll(key, HEAD // 2, 1) * sine
            kv_ref[0, g] = key.astype(BF16)
            kv_ref[1, g] = part[:, 2 * HEAD :]
        out_ref[...] = jnp.zeros_like(out_ref)

    wide = QUAD * STEPS * HEADS
    row, col = iota((QUAD * TOKENS, wide), 0), iota((QUAD * TOKENS, wide), 1)
    own = (
        (row // TOKENS == (col % 16) // STEPS)
        & (row % TOKENS // 32 == col // 16)
        & (col % STEPS <= row % STEPS)
    )
    tall = iota((QUAD * TOKENS, 1), 0)
    groups = range(FRESH_BLOCK // QUAD)
    fresh = [
        [
            jnp.concatenate(
                [
                    kv_ref[
                        kind,
                        g,
                        pl.ds(pl.multiple_of((step * len(groups) + n) * 16, 16), 16),
                    ]
                    for g in range(HEADS)
                ],
                axis=0,
            )
            for n in groups
        ]
        for kind in range(2)
    ]

    def rows(ref, n):
        return ref[n * QUAD : (n + 1) * QUAD].reshape(QUAD * TOKENS, HEAD)

    score = [
        lax.dot_general(
            rows(qp_ref, n), fresh[0][n], (((1,), (1,)), ((), ())), preferred_element_type=F32
        )
        for n in groups
    ]
    score = [jnp.where(own, s * SCALE, masked_score) for s in score]
    lse = [rows(lse_ref, n)[:, :1] for n in groups]
    top = [jnp.maximum(jnp.max(s, axis=1, keepdims=True), old) for s, old in zip(score, lse)]
    weight = [jnp.exp(s - t) for s, t in zip(score, top)]
    share = [jnp.exp(old - t) for old, t in zip(lse, top)]
    total = [jnp.sum(w, axis=1, keepdims=True) + a for w, a in zip(weight, share)]
    for n in groups:
        first = step * FRESH_BLOCK + n * QUAD
        length = lengths[first]
        for k in range(1, QUAD):
            length = jnp.where(tall < k * TOKENS, length, lengths[first + k])
        kept = (tall % STEPS) < length
        scale = jnp.where(kept, 1.0 / total[n], 0.0)
        mixed = (share[n] * scale) * rows(old_ref, n) + jnp.dot(
            (weight[n] * scale).astype(BF16), fresh[1][n], preferred_element_type=F32
        )
        mixed = mixed.astype(BF16)
        for k in range(QUAD):
            out_ref[dest[first + k], slot[first + k]] = mixed[k * TOKENS : (k + 1) * TOKENS]


def fresh(dest, slot, lengths, me, parts, cosine, sine, queries, lse, old):
    def whole_block(shape):
        return pl.BlockSpec(shape, lambda i, *_: (0,) * len(shape))

    inside = pl.BlockSpec((FRESH_BLOCK, TOKENS, HEAD), lambda i, *_: (i, 0, 0))
    kv = (2, HEADS, TOKENS, HEAD)
    out = (N_FSDP, SLOTS, TOKENS, HEAD)
    return pl.pallas_call(
        fresh_kernel,
        grid_spec=pltpu.PrefetchScalarGridSpec(
            num_scalar_prefetch=4,
            grid=(ROLL // FRESH_BLOCK,),
            in_specs=[whole_block((TOKENS, 3 * HEAD))] * 4
            + [whole_block((TOKENS, HEAD))] * 2
            + [inside] * 3,
            out_specs=(whole_block(kv), whole_block(out)),
        ),
        out_shape=(jax.ShapeDtypeStruct(kv, BF16), jax.ShapeDtypeStruct(out, BF16)),
        compiler_params=params(),
        cost_estimate=SMALL,
        name="fresh",
    )(dest, slot, lengths, me, *parts, cosine, sine, queries, lse, old)


def in_rows(joined):
    joined = joined.reshape(N_FSDP, SLOTS, 8 * HEADS, STEPS, HEAD).transpose(0, 1, 3, 2, 4)
    return joined.reshape(1, 1, N_FSDP, SLOTS, STEPS, 8 * HEADS * HEAD)


def turn_tables(prefix_lengths):
    half_size = HEAD // 2
    exponent = -2.0 * jnp.arange(half_size).astype(F32) / HEAD
    inverse_freq = jnp.power(jnp.float32(rope_theta), exponent)
    positions = prefix_lengths[:, None] + jnp.arange(STEPS, dtype=jnp.int32)[None, :]
    angle = positions.reshape(TOKENS, 1).astype(F32) * inverse_freq
    cosine, sine = jnp.cos(angle), jnp.sin(angle)
    return (
        jnp.concatenate([cosine, cosine], axis=-1),
        jnp.concatenate([-sine, sine], axis=-1),
    )


def along(moves):
    def place_of(x):
        return (x % 2) * 2 + x // 2

    return [(place_of(start), place_of(stop)) for start, stop in moves]


def shift_y(k):
    return [(y, (y + k) % N_Y) for y in range(N_Y)]


def on_device(
    master_weight,
    gradient,
    first_moment,
    second_moment,
    new_inputs,
    queries,
    cache_keys,
    cache_values,
    prefix_lengths,
    rollout_lengths,
    destinations,
):
    new_master, new_first, new_second, blocks = adam(
        master_weight, gradient, first_moment, second_moment
    )
    own_rows = lax.all_to_all(
        blocks.reshape(N_Z * N_GEN, ROWS, 2 * HEAD), ("z", "xl", "c"), 0, 0, tiled=True
    ).reshape(DEPTH, 2 * HEAD)

    core = [(0, 1), (1, 0)]
    own, low, high = columns(new_inputs, blocks)
    right = [(x, (x + 1) % 4) for x in range(4)]
    left = [(x, (x + 3) % 4) for x in range(4)]
    near = lax.ppermute(own, "c", core)
    far_a = lax.ppermute(low, ("xl", "tp"), along(right))
    far_b = lax.ppermute(high, ("xl", "tp"), along(left))
    both_a, both_b = (lax.ppermute(far, "c", core) for far in (far_a, far_b))
    inputs = (own, near, far_a, far_b, both_a, both_b)

    same_dest = destinations[:, None] == destinations[None, :]
    earlier = jnp.arange(ROLL)[None, :] < jnp.arange(ROLL)[:, None]
    slot_rank = jnp.sum((same_dest & earlier).astype(jnp.int32), axis=1)
    old_rows, lse, ordered = old_attention(
        prefix_lengths,
        queries.reshape(ROLL, TOKENS, HEAD),
        cache_keys.reshape(ROLL, CACHE * HEADS, HEAD),
        cache_values.reshape(ROLL, CACHE * HEADS, HEAD),
        own,
    )
    own_rows = after(own_rows, lse)
    me = jnp.stack([lax.axis_index("y"), lax.axis_index("xl") * 2 + lax.axis_index("c")])
    before = lax.ppermute(own_rows, "y", shift_y(1))
    beyond = lax.ppermute(own_rows, "y", shift_y(-1))
    total = project(me, (0,), (own_rows,), inputs[:2], None, False)
    low, high = halves(before, beyond, total)
    across = [lax.ppermute(low, "y", shift_y(1)), lax.ppermute(high, "y", shift_y(-1))]
    total = project(me, (0, 1, 3), (own_rows, before, beyond), inputs, total, False)
    parts = project(me, (2, 2), across, inputs, total, True)
    parts = [parts[0]] + [
        lax.ppermute(parts[j], ("xl", "c"), [(q, q ^ j) for q in range(N_GEN)]) for j in (1, 2, 3)
    ]
    cosine, sine = turn_tables(prefix_lengths)
    fresh_parts, rows = fresh(
        destinations, slot_rank, rollout_lengths, me, parts, cosine, sine, ordered, lse, old_rows
    )
    rows = lax.all_to_all(rows, ("y", "z"), 0, 0, tiled=True)
    fresh_kv = fresh_parts.reshape(2, HEADS, ROLL, STEPS, HEAD).transpose(2, 3, 0, 1, 4)
    returned_rows = in_rows(rows)
    return (new_master, new_first, new_second, fresh_kv, returned_rows)


def solution(mesh):
    fine = Mesh(mesh.devices.reshape(N_Y, N_Z, 2, 2, 2), ("y", "z", "xl", "c", "tp"))
    group = ("y", "z", "xl", "c")
    rows = P(None, group, "tp")
    in_specs = (
        rows,
        rows,
        rows,
        rows,
        P(group, None, None),
        P(group, None, "tp", None),
        P(group, None, "tp", None),
        P(group, None, "tp", None),
        P(group),
        P(group),
        P(group),
    )
    out_specs = (
        rows,
        rows,
        rows,
        P(group, None, None, "tp", None),
        P(("y", "z"), ("xl", "c"), None, None, None, "tp"),
    )
    return jax.shard_map(
        on_device, mesh=fine, in_specs=in_specs, out_specs=out_specs, check_vma=False
    )
```

```python
import functools
import jax
import jax.numpy as jnp
from jax import lax
from jax.experimental import pallas as pl
from jax.experimental.pallas import tpu as pltpu
from jax.sharding import Mesh, PartitionSpec as P

beta_one = 0.9
beta_two = 0.95
adam_eps = 1e-08
learn_rate = 0.002
weight_decay = 0.1
adam_step = 10.0
rope_theta = 1000000.0
norm_eps = 1e-06
masked_score = -1e30

N_Y = 4
N_Z = 8
N_GEN = 4
N_FSDP = N_Y * N_Z
HEAD = 128
HEADS = 4
STEPS = 4
ROLL = 32
TOKENS = ROLL * STEPS
CACHE = 128
ROWS = 40
DEPTH = 1280
SLOTS = 2
SCALE = HEAD ** (-0.5)
F32 = jnp.float32
BF16 = jnp.bfloat16
VMEM_BYTES = 40 * 1024 * 1024
VMEM_MOST = 60 * 1024 * 1024


SMALL = pl.CostEstimate(flops=1000, bytes_accessed=1000, transcendentals=0)


def params(limit=VMEM_BYTES):
    return pltpu.CompilerParams(vmem_limit_bytes=limit)


def whole():
    return pl.BlockSpec(memory_space=pltpu.VMEM)


def iota(shape, axis):
    return lax.broadcasted_iota(jnp.int32, shape, axis)


def after(value, *others):
    anywhere = pl.BlockSpec(memory_space=pl.ANY)
    return pl.pallas_call(
        lambda *refs: None,
        in_specs=[anywhere] * (1 + len(others)),
        out_specs=anywhere,
        out_shape=jax.ShapeDtypeStruct(value.shape, value.dtype),
        input_output_aliases={0: 0},
        cost_estimate=SMALL,
        name="after",
    )(value, *others)


def adam_kernel(*refs):
    sources, (m_out, f_out, s_out, w_out) = refs[:4], refs[4:8]
    held, sems = refs[8], refs[9]
    copies = [
        pltpu.make_async_copy(source, held.at[i], sems.at[i]) for i, source in enumerate(sources)
    ]
    for copy in copies:
        copy.start()
    for copy in copies:
        copy.wait()
    for kv in range(2):
        master, grad, first, second = (held[i, kv] for i in range(4))
        first = beta_one * first + (1.0 - beta_one) * grad
        second = beta_two * second + (1.0 - beta_two) * grad * grad
        first_hat = first / (1.0 - beta_one**adam_step)
        second_hat = second / (1.0 - beta_two**adam_step)
        master = master - learn_rate * (
            first_hat / (jnp.sqrt(second_hat) + adam_eps) + weight_decay * master
        )
        f_out[kv] = first
        s_out[kv] = second
        m_out[kv] = master
        rounded = master.astype(BF16)
        for q in range(N_GEN):
            piece = rounded[:, q * HEAD : (q + 1) * HEAD]
            for z in range(N_Z):
                w_out[z, q, :, kv * HEAD : (kv + 1) * HEAD] = piece


def adam(master, grad, first, second):
    shape = jax.ShapeDtypeStruct(master.shape, F32)
    return pl.pallas_call(
        adam_kernel,
        out_shape=(shape, shape, shape, jax.ShapeDtypeStruct((N_Z, N_GEN, ROWS, 2 * HEAD), BF16)),
        in_specs=[pl.BlockSpec(memory_space=pl.ANY)] * 4,
        out_specs=(whole(),) * 4,
        scratch_shapes=[
            pltpu.VMEM((4,) + master.shape, F32),
            pltpu.SemaphoreType.DMA((4,)),
        ],
        compiler_params=params(VMEM_MOST),
        cost_estimate=SMALL,
        name="adam",
    )(master, grad, first, second)


def columns_kernel(x_ref, _, out_ref, low_ref, high_ref):
    block = x_ref[...].reshape(TOKENS, DEPTH)
    out_ref[0] = block
    low_ref[0] = block[: TOKENS // 2]
    high_ref[0] = block[TOKENS // 2 :]


def columns(inputs, later):
    def shape(rows):
        return jax.ShapeDtypeStruct((N_Y, rows, DEPTH), BF16)

    def block(rows):
        return pl.BlockSpec((1, rows, DEPTH), lambda i: (i, 0, 0))

    return pl.pallas_call(
        columns_kernel,
        grid=(N_Y,),
        in_specs=[
            pl.BlockSpec((ROLL, STEPS, DEPTH), lambda i: (0, 0, i)),
            pl.BlockSpec(memory_space=pl.ANY),
        ],
        out_specs=(block(TOKENS), block(TOKENS // 2), block(TOKENS // 2)),
        out_shape=(shape(TOKENS), shape(TOKENS // 2), shape(TOKENS // 2)),
        compiler_params=params(),
        cost_estimate=SMALL,
        name="columns",
    )(inputs, later)


OLD_BLOCK = 8
PIECE = TOKENS // N_Y
LOG2E = 1.4426950408889634


def old_kernel(prefix, q_ref, k_ref, v_ref, _, out_ref, lse_ref, qp_ref, bias_ref):
    step = pl.program_id(0)
    span = CACHE * HEADS
    block = range(OLD_BLOCK)

    @pl.when(step == 0)
    def _():
        row, col = iota((TOKENS, span), 0), iota((TOKENS, span), 1)
        bias_ref[...] = jnp.where(col % HEADS == row // 32, 0.0, masked_score)

    row, col = iota((TOKENS, TOKENS), 0), iota((TOKENS, TOKENS), 1)
    perm = ((col % 32 == row // 4) & (col // 32 == row % 4)).astype(BF16)
    lane = iota((1, span), 1)
    query = [
        jnp.dot(perm, q_ref[n], preferred_element_type=F32).astype(BF16) for n in block
    ]
    for n in block:
        qp_ref[n] = query[n]
    score = [
        lax.dot_general(
            query[n], k_ref[n], (((1,), (1,)), ((), ())), preferred_element_type=F32
        )
        for n in block
    ]
    score = [
        score[n]
        + bias_ref[...]
        + jnp.where(lane < prefix[step * OLD_BLOCK + n] * HEADS, 0.0, masked_score)
        for n in block
    ]
    top = [jnp.max(s, axis=1, keepdims=True) for s in score]
    weight = [jnp.exp2((s - t) * (SCALE * LOG2E)) for s, t in zip(score, top)]
    total = [jnp.sum(w, axis=1, keepdims=True) for w in weight]
    mixed = [
        jnp.dot(weight[n].astype(BF16), v_ref[n], preferred_element_type=F32) for n in block
    ]
    for n in block:
        out_ref[n] = mixed[n] * (1.0 / total[n])
        lse_ref[n] = jnp.broadcast_to(top[n] * SCALE + jnp.log(total[n]), (TOKENS, HEAD))


def old_attention(prefix, queries, keys, values, later):
    span = CACHE * HEADS
    inside = pl.BlockSpec((OLD_BLOCK, TOKENS, HEAD), lambda i, *_: (i, 0, 0))
    cache = pl.BlockSpec((OLD_BLOCK, span, HEAD), lambda i, *_: (i, 0, 0))
    rows = (ROLL, TOKENS, HEAD)
    return pl.pallas_call(
        old_kernel,
        grid_spec=pltpu.PrefetchScalarGridSpec(
            num_scalar_prefetch=1,
            grid=(ROLL // OLD_BLOCK,),
            in_specs=[inside, cache, cache, pl.BlockSpec(memory_space=pl.ANY)],
            out_specs=(inside, inside, inside),
            scratch_shapes=[pltpu.VMEM((TOKENS, span), F32)],
        ),
        out_shape=(
            jax.ShapeDtypeStruct(rows, F32),
            jax.ShapeDtypeStruct(rows, F32),
            jax.ShapeDtypeStruct(rows, BF16),
        ),
        compiler_params=params(VMEM_MOST),
        cost_estimate=SMALL,
        name="old_attention",
    )(prefix, queries, keys, values, later)


def halves_kernel(before, beyond, _, low, high):
    half = DEPTH // 2
    low[...] = before[:half]
    high[...] = beyond[half:]


def halves(before, beyond, later):
    shape = jax.ShapeDtypeStruct((DEPTH // 2, 2 * HEAD), BF16)
    return pl.pallas_call(
        halves_kernel,
        in_specs=[whole(), whole(), pl.BlockSpec(memory_space=pl.ANY)],
        out_specs=(whole(),) * 2,
        out_shape=(shape,) * 2,
        compiler_params=params(),
        cost_estimate=SMALL,
        name="halves",
    )(before, beyond, later)


def project_kernel(shifts, sources, carried, last, me, *refs):
    weights, refs = refs[: len(shifts)], refs[len(shifts) :]
    count = 2 if sources == 2 else 6
    own, near, *far = refs[:count]
    out_ref = refs[-1]
    half = TOKENS // 2
    places = [(own, 0, 0, TOKENS), (near, 1, 0, TOKENS)]
    for n, ref in enumerate(far):
        places.append((ref, 2 + n // 2, n % 2 * half, n % 2 * half + half))
    for ref, j, start, stop in places:
        total = refs[count][j, start:stop] if j < carried else None
        at = 0
        for n, (shift, weight) in enumerate(zip(shifts, weights)):
            if n == 0 and j < carried and shift == 0:
                continue
            part = (me[0] + (N_Y - shift)) % N_Y
            depth = weight.shape[0]
            term = jnp.dot(ref[part, :, at : at + depth], weight[...], preferred_element_type=F32)
            total = term if total is None else total + term
            at = (at + depth) % DEPTH
        if last:
            key, value = total[:, :HEAD], total[:, HEAD:]
            high = key.astype(BF16)
            out_ref[j, start:stop, :HEAD] = high
            out_ref[j, start:stop, HEAD : 2 * HEAD] = (key - high.astype(F32)).astype(BF16)
            out_ref[j, start:stop, 2 * HEAD :] = value.astype(BF16)
        else:
            out_ref[j, start:stop] = total


def project(me, shifts, weights, inputs, total, last, *later):
    width, dtype = (3 * HEAD, BF16) if last else (2 * HEAD, F32)
    sources = 2 if len(inputs) == 2 else N_GEN
    carried = () if total is None else (total,)
    return pl.pallas_call(
        functools.partial(
            project_kernel, shifts, sources, 0 if total is None else total.shape[0], last
        ),
        in_specs=[pl.BlockSpec(memory_space=pltpu.SMEM)]
        + [whole()] * (len(weights) + len(inputs) + len(carried))
        + [pl.BlockSpec(memory_space=pl.ANY)] * len(later),
        out_specs=whole(),
        out_shape=jax.ShapeDtypeStruct((sources, TOKENS, width), dtype),
        compiler_params=params(),
        cost_estimate=SMALL,
        name="project",
    )(me, *weights, *inputs, *carried, *later)


FRESH_BLOCK = 16
QUAD = 4


def fresh_kernel(
    dest, slot, lengths, me, p0, p1, p2, p3, cos_ref, sin_ref, qp_ref, lse_ref, old_ref,
    q_one, lse_one, *refs,
):
    kv_ref, out_ref, more_ref = refs[-3:]
    step = ROLL // FRESH_BLOCK - 1 - pl.program_id(0)

    @pl.when(pl.program_id(0) == 0)
    def _():
        cosine, sine = cos_ref[...], sin_ref[...]
        for j, part in enumerate((p0, p1, p2, p3)):
            g = me[1] ^ j
            key = part[:, :HEAD].astype(F32) + part[:, HEAD : 2 * HEAD].astype(F32)
            key = key / jnp.sqrt(jnp.mean(key * key, axis=-1, keepdims=True) + norm_eps)
            key = key * cosine + pltpu.roll(key, HEAD // 2, 1) * sine
            kv_ref[0, g] = key.astype(BF16)
            kv_ref[1, g] = part[:, 2 * HEAD :]
        out_ref[...] = jnp.zeros_like(out_ref)
        more_ref[...] = jnp.zeros_like(more_ref)
        late_rows(me, dest, slot, lengths, q_one, lse_one, kv_ref, out_ref)

    wide = QUAD * STEPS * HEADS
    row, col = iota((QUAD * TOKENS, wide), 0), iota((QUAD * TOKENS, wide), 1)
    own = (
        (row // TOKENS == (col % 16) // STEPS)
        & (row % TOKENS // 32 == col // 16)
        & (col % STEPS <= row % STEPS)
    )
    tall = iota((QUAD * TOKENS, 1), 0)
    groups = range(FRESH_BLOCK // QUAD)
    fresh = [
        [
            jnp.concatenate(
                [
                    kv_ref[
                        kind,
                        g,
                        pl.ds(pl.multiple_of((step * len(groups) + n) * 16, 16), 16),
                    ]
                    for g in range(HEADS)
                ],
                axis=0,
            )
            for n in groups
        ]
        for kind in range(2)
    ]

    def rows(ref, n):
        return ref[n * QUAD : (n + 1) * QUAD].reshape(QUAD * TOKENS, HEAD)

    score = [
        lax.dot_general(
            rows(qp_ref, n), fresh[0][n], (((1,), (1,)), ((), ())), preferred_element_type=F32
        )
        for n in groups
    ]
    score = [jnp.where(own, s * SCALE, masked_score) for s in score]
    lse = [rows(lse_ref, n)[:, :1] for n in groups]
    top = [jnp.maximum(jnp.max(s, axis=1, keepdims=True), old) for s, old in zip(score, lse)]
    weight = [jnp.exp(s - t) for s, t in zip(score, top)]
    share = [jnp.exp(old - t) for old, t in zip(lse, top)]
    total = [jnp.sum(w, axis=1, keepdims=True) + a for w, a in zip(weight, share)]
    for n in reversed(groups):
        first = step * FRESH_BLOCK + n * QUAD
        length = lengths[first]
        for k in range(1, QUAD):
            length = jnp.where(tall < k * TOKENS, length, lengths[first + k])
        kept = (tall % STEPS) < length
        scale = jnp.where(kept, 1.0 / total[n], 0.0)
        mixed = (share[n] * scale) * rows(old_ref, n) + jnp.dot(
            (weight[n] * scale).astype(BF16), fresh[1][n], preferred_element_type=F32
        )
        mixed = mixed.astype(BF16)
        for k in reversed(range(QUAD)):
            d, j = dest[first + k], slot[first + k]
            row = mixed[k * TOKENS : (k + 1) * TOKENS]
            out_ref[d, :TOKENS] = row
            more_ref[jnp.where(j == 1, d, N_FSDP)] = row


def late_rows(me, dest, slot, lengths, q_one, lse_one, kv_ref, out_ref):
    r = me[2]
    start = pl.multiple_of(r // QUAD * 16, 16)
    keys, values = (
        jnp.concatenate([kv_ref[kind, g, pl.ds(start, 16)] for g in range(HEADS)], axis=0)
        for kind in range(2)
    )
    score = lax.dot_general(
        keys, q_one[0], (((1,), (1,)), ((), ())), preferred_element_type=F32
    )
    row, lane = iota((64, TOKENS), 0), iota((64, TOKENS), 1)
    own = (
        (row // 16 == lane // 32)
        & (row % 16 // STEPS == r % QUAD)
        & (row % STEPS <= lane % STEPS)
    )
    score = jnp.where(own, score * SCALE, masked_score)
    eye = iota((TOKENS, TOKENS), 0) == iota((TOKENS, TOKENS), 1)
    old = jnp.sum(jnp.where(eye, lse_one[0], 0.0), axis=0, keepdims=True)
    top = jnp.maximum(jnp.max(score, axis=0, keepdims=True), old)
    weight, share = jnp.exp(score - top), jnp.exp(old - top)
    total = jnp.sum(weight, axis=0, keepdims=True) + share
    kept = (iota((1, TOKENS), 1) % STEPS) < lengths[r]
    scale = jnp.where(kept, 1.0 / total, 0.0)
    weight, share = weight * scale, share * scale
    rows = weight[0:8]
    for n in range(8, 64, 8):
        rows = rows + weight[n : n + 8]
    rows = rows + pltpu.roll(rows, 4, 0)
    place = iota((8, TOKENS), 0)
    rows = jnp.where(place < 4, rows, jnp.where(place == 4, share, 0.0))
    rows = jnp.concatenate([rows, jnp.zeros_like(rows)], axis=0)
    pick = (
        iota((16, 64), 1) == iota((16, 64), 0) // 4 * 16 + r % QUAD * 4 + iota((16, 64), 0) % 4
    ).astype(BF16)
    values = jnp.dot(pick, values, preferred_element_type=F32).astype(BF16)
    seconds = lax.fori_loop(0, ROLL, lambda n, a: a + (slot[n] > 0).astype(jnp.int32), 0)
    count = jnp.where(iota((16, TOKENS), 0) == 5, seconds.astype(F32), 0.0)
    for d in range(N_FSDP):
        out_ref[d, TOKENS + 16 :] = count.astype(BF16)
    d = dest[r]
    out_ref[d, TOKENS : TOKENS + 16] = values
    out_ref[d, TOKENS + 16 :] = (rows + count).astype(BF16)


def fresh(dest, slot, lengths, me, parts, cosine, sine, queries, lse, old):
    def whole_block(shape):
        return pl.BlockSpec(shape, lambda i, *_: (0,) * len(shape))

    steps = ROLL // FRESH_BLOCK
    inside = pl.BlockSpec((FRESH_BLOCK, TOKENS, HEAD), lambda i, *_: (steps - 1 - i, 0, 0))
    one = pl.BlockSpec((1, TOKENS, HEAD), lambda i, dest, slot, lengths, me: (me[2], 0, 0))
    kv = (2, HEADS, TOKENS, HEAD)
    out = (N_FSDP, TOKENS + 32, HEAD)
    more = (N_FSDP + 1, TOKENS, HEAD)
    return pl.pallas_call(
        fresh_kernel,
        grid_spec=pltpu.PrefetchScalarGridSpec(
            num_scalar_prefetch=4,
            grid=(steps,),
            in_specs=[whole_block((TOKENS, 3 * HEAD))] * 4
            + [whole_block((TOKENS, HEAD))] * 2
            + [inside] * 3
            + [one] * 2,
            out_specs=(whole_block(kv), whole_block(out), whole_block(more)),
        ),
        out_shape=tuple(jax.ShapeDtypeStruct(shape, BF16) for shape in (kv, out, more)),
        compiler_params=params(),
        cost_estimate=SMALL,
        name="fresh",
    )(dest, slot, lengths, me, *parts, cosine, sine, queries, lse, old, queries, lse)


def second_kernel(me, old_ref, _, out_ref):
    row = old_ref[0].astype(BF16)
    for z in range(N_Z):
        out_ref[z] = row


def second(me, old, later):
    return pl.pallas_call(
        second_kernel,
        grid_spec=pltpu.PrefetchScalarGridSpec(
            num_scalar_prefetch=1,
            grid=(1,),
            in_specs=[
                pl.BlockSpec((1, TOKENS, HEAD), lambda i, me: (me[2], 0, 0)),
                pl.BlockSpec(memory_space=pl.ANY),
            ],
            out_specs=pl.BlockSpec((N_Z, TOKENS, HEAD), lambda i, me: (0, 0, 0)),
        ),
        out_shape=jax.ShapeDtypeStruct((N_Z, TOKENS, HEAD), BF16),
        compiler_params=params(),
        cost_estimate=SMALL,
        name="second",
    )(me, old, later)


def join_kernel(me, in_ref, e0, e1, e2, e3, _, out_ref, most_ref, seen_ref):
    step = pl.program_id(0)

    @pl.when(step == 0)
    def _():
        seen_ref[...] = jnp.zeros_like(seen_ref)

    eye = iota((TOKENS, TOKENS), 0) == iota((TOKENS, TOKENS), 1)
    row8 = iota((8, 128), 0)
    same = iota((16, 128), 1) // 32 == iota((16, 128), 0) // 4
    block = range(N_Z)

    def body(extra):
        for n in block:
            out_ref[n, 0] = in_ref[n, :TOKENS]
        tiles = [in_ref[n, TOKENS + 16 :, :].astype(F32)[:8] for n in block]
        most = tiles[0]
        for tile in tiles[1:]:
            most = jnp.maximum(most, tile)
        seen_ref[...] = jnp.maximum(seen_ref[...], most)
        diags = [jnp.where(eye, tile[4:5], 0.0).astype(BF16) for tile in tiles]
        both = [jnp.where(row8 < 4, tile, pltpu.roll(tile, 4, 0)) for tile in tiles]
        weights = [
            jnp.where(same, jnp.concatenate([w, w], axis=0), 0.0).astype(BF16) for w in both
        ]
        kept = [
            jnp.dot(diags[n], extra[n], preferred_element_type=F32) for n in block
        ]
        added = [
            lax.dot_general(
                weights[n],
                in_ref[n, TOKENS : TOKENS + 16, :],
                (((0,), (0,)), ((), ())),
                preferred_element_type=F32,
            )
            for n in block
        ]
        for n in block:
            out_ref[n, 1] = (kept[n] + added[n]).astype(BF16)

    for k, extra in enumerate((e0, e1, e2, e3)):
        pl.when(step == k)(functools.partial(body, extra))

    @pl.when(step == pl.num_programs(0) - 1)
    def _():
        most_ref[0] = jnp.max(seen_ref[5:6, :]).astype(jnp.int32)


def join(me, rows, extras, later):
    def of_source(i, me):
        return (me[0] + N_Y - i) % N_Y

    return pl.pallas_call(
        join_kernel,
        grid_spec=pltpu.PrefetchScalarGridSpec(
            num_scalar_prefetch=1,
            grid=(N_Y,),
            in_specs=[pl.BlockSpec((N_Z, TOKENS + 32, HEAD), lambda i, me: (of_source(i, me), 0, 0))]
            + [pl.BlockSpec((N_Z, TOKENS, HEAD), lambda i, me: (0, 0, 0))] * 4
            + [pl.BlockSpec(memory_space=pl.ANY)],
            out_specs=(
                pl.BlockSpec(
                    (N_Z, SLOTS, TOKENS, HEAD), lambda i, me: (of_source(i, me), 0, 0, 0)
                ),
                pl.BlockSpec(memory_space=pltpu.SMEM),
            ),
            scratch_shapes=[pltpu.VMEM((8, HEAD), F32)],
        ),
        out_shape=(
            jax.ShapeDtypeStruct((N_FSDP, SLOTS, TOKENS, HEAD), BF16),
            jax.ShapeDtypeStruct((1,), jnp.int32),
        ),
        compiler_params=params(),
        cost_estimate=SMALL,
        name="join",
    )(me, rows, *extras, later)


def in_rows(joined):
    joined = joined.reshape(N_FSDP, SLOTS, 8 * HEADS, STEPS, HEAD).transpose(0, 1, 3, 2, 4)
    return joined.reshape(1, 1, N_FSDP, SLOTS, STEPS, 8 * HEADS * HEAD)


def turn_tables(prefix_lengths):
    half_size = HEAD // 2
    exponent = -2.0 * jnp.arange(half_size).astype(F32) / HEAD
    inverse_freq = jnp.power(jnp.float32(rope_theta), exponent)
    positions = prefix_lengths[:, None] + jnp.arange(STEPS, dtype=jnp.int32)[None, :]
    angle = positions.reshape(TOKENS, 1).astype(F32) * inverse_freq
    cosine, sine = jnp.cos(angle), jnp.sin(angle)
    return (
        jnp.concatenate([cosine, cosine], axis=-1),
        jnp.concatenate([-sine, sine], axis=-1),
    )


def along(moves):
    def place_of(x):
        return (x % 2) * 2 + x // 2

    return [(place_of(start), place_of(stop)) for start, stop in moves]


def shift_y(k):
    return [(y, (y + k) % N_Y) for y in range(N_Y)]


def on_device(
    master_weight,
    gradient,
    first_moment,
    second_moment,
    new_inputs,
    queries,
    cache_keys,
    cache_values,
    prefix_lengths,
    rollout_lengths,
    destinations,
):
    new_master, new_first, new_second, blocks = adam(
        master_weight, gradient, first_moment, second_moment
    )
    own_rows = lax.all_to_all(
        blocks.reshape(N_Z * N_GEN, ROWS, 2 * HEAD), ("z", "xl", "c"), 0, 0, tiled=True
    ).reshape(DEPTH, 2 * HEAD)

    core = [(0, 1), (1, 0)]
    own, low, high = columns(new_inputs, blocks)
    right = [(x, (x + 1) % 4) for x in range(4)]
    left = [(x, (x + 3) % 4) for x in range(4)]
    near = lax.ppermute(own, "c", core)
    far_a = lax.ppermute(low, ("xl", "tp"), along(right))
    far_b = lax.ppermute(high, ("xl", "tp"), along(left))
    both_a, both_b = (lax.ppermute(far, "c", core) for far in (far_a, far_b))
    inputs = (own, near, far_a, far_b, both_a, both_b)

    same_dest = destinations[:, None] == destinations[None, :]
    earlier = jnp.arange(ROLL)[None, :] < jnp.arange(ROLL)[:, None]
    slot_rank = jnp.sum((same_dest & earlier).astype(jnp.int32), axis=1)
    old_rows, lse, ordered = old_attention(
        prefix_lengths,
        queries.reshape(ROLL, TOKENS, HEAD),
        cache_keys.reshape(ROLL, CACHE * HEADS, HEAD),
        cache_values.reshape(ROLL, CACHE * HEADS, HEAD),
        own,
    )
    own_rows = after(own_rows, lse)
    one = jnp.argmax(slot_rank).astype(jnp.int32)
    me = jnp.stack([lax.axis_index("y"), lax.axis_index("xl") * 2 + lax.axis_index("c"), one])
    before = lax.ppermute(own_rows, "y", shift_y(1))
    beyond = lax.ppermute(own_rows, "y", shift_y(-1))
    total = project(me, (0,), (own_rows,), inputs[:2], None, False)
    extra = lax.all_to_all(second(me, old_rows, total), "z", 0, 0, tiled=True)
    low, high = halves(before, beyond, total)
    across = [lax.ppermute(low, "y", shift_y(1)), lax.ppermute(high, "y", shift_y(-1))]
    total = project(me, (0, 1, 3), (own_rows, before, beyond), inputs, total, False)
    parts = project(me, (2, 2), across, inputs, total, True, extra)
    parts = [parts[0]] + [
        lax.ppermute(parts[j], ("xl", "c"), [(q, q ^ j) for q in range(N_GEN)]) for j in (1, 2, 3)
    ]
    cosine, sine = turn_tables(prefix_lengths)
    fresh_parts, rows, more = fresh(
        destinations, slot_rank, rollout_lengths, me, parts, cosine, sine, ordered, lse, old_rows
    )
    rows = lax.all_to_all(rows, ("y", "z"), 0, 0, tiled=True)
    extras = [extra] + [lax.ppermute(extra, "y", shift_y(k)) for k in (1, 2, 3)]
    fresh_kv = fresh_parts.reshape(2, HEADS, ROLL, STEPS, HEAD).transpose(2, 3, 0, 1, 4)
    joined, most = join(me, rows, extras, fresh_kv)

    def with_all_seconds():
        seconds = lax.all_to_all(more[:N_FSDP], ("y", "z"), 0, 0, tiled=True)
        return jnp.stack([joined[:, 0], seconds], axis=1)

    returned_rows = in_rows(after(lax.cond(most[0] > 1, with_all_seconds, lambda: joined)))
    return (new_master, new_first, new_second, fresh_kv, returned_rows)


def solution(mesh):
    fine = Mesh(mesh.devices.reshape(N_Y, N_Z, 2, 2, 2), ("y", "z", "xl", "c", "tp"))
    group = ("y", "z", "xl", "c")
    rows = P(None, group, "tp")
    in_specs = (
        rows,
        rows,
        rows,
        rows,
        P(group, None, None),
        P(group, None, "tp", None),
        P(group, None, "tp", None),
        P(group, None, "tp", None),
        P(group),
        P(group),
        P(group),
    )
    out_specs = (
        rows,
        rows,
        rows,
        P(group, None, None, "tp", None),
        P(("y", "z"), ("xl", "c"), None, None, None, "tp"),
    )
    return jax.shard_map(
        on_device, mesh=fine, in_specs=in_specs, out_specs=out_specs, check_vma=False
    )
```

```python
import functools
import jax
import jax.numpy as jnp
from jax import lax
from jax.experimental import pallas as pl
from jax.experimental.pallas import tpu as pltpu
from jax.sharding import Mesh, PartitionSpec as P

beta_one = 0.9
beta_two = 0.95
adam_eps = 1e-08
learn_rate = 0.002
weight_decay = 0.1
adam_step = 10.0
rope_theta = 1000000.0
norm_eps = 1e-06
masked_score = -1e30

N_Y = 4
N_Z = 8
N_GEN = 4
N_FSDP = N_Y * N_Z
HEAD = 128
HEADS = 4
STEPS = 4
ROLL = 32
TOKENS = ROLL * STEPS
CACHE = 128
ROWS = 40
DEPTH = 1280
SLOTS = 2
SCALE = HEAD ** (-0.5)
F32 = jnp.float32
BF16 = jnp.bfloat16
VMEM_BYTES = 40 * 1024 * 1024
VMEM_MOST = 60 * 1024 * 1024
VMEM_LEAST = 16 * 1024 * 1024


SMALL = pl.CostEstimate(flops=1000, bytes_accessed=1000, transcendentals=0)


def params(limit=VMEM_BYTES):
    return pltpu.CompilerParams(vmem_limit_bytes=limit)


def whole():
    return pl.BlockSpec(memory_space=pltpu.VMEM)


def iota(shape, axis):
    return lax.broadcasted_iota(jnp.int32, shape, axis)


def after(value, *others):
    anywhere = pl.BlockSpec(memory_space=pl.ANY)
    return pl.pallas_call(
        lambda *refs: None,
        in_specs=[anywhere] * (1 + len(others)),
        out_specs=anywhere,
        out_shape=jax.ShapeDtypeStruct(value.shape, value.dtype),
        input_output_aliases={0: 0},
        cost_estimate=SMALL,
        name="after",
    )(value, *others)


def adam_kernel(*refs):
    sources, (m_out, f_out, s_out, w_out) = refs[:4], refs[4:8]
    held, sems = refs[8], refs[9]
    copies = [
        pltpu.make_async_copy(source, held.at[i], sems.at[i]) for i, source in enumerate(sources)
    ]
    for copy in copies:
        copy.start()
    for copy in copies:
        copy.wait()
    for kv in range(2):
        master, grad, first, second = (held[i, kv] for i in range(4))
        first = beta_one * first + (1.0 - beta_one) * grad
        second = beta_two * second + (1.0 - beta_two) * grad * grad
        first_hat = first / (1.0 - beta_one**adam_step)
        second_hat = second / (1.0 - beta_two**adam_step)
        master = master - learn_rate * (
            first_hat / (jnp.sqrt(second_hat) + adam_eps) + weight_decay * master
        )
        f_out[kv] = first
        s_out[kv] = second
        m_out[kv] = master
        rounded = master.astype(BF16)
        for q in range(N_GEN):
            piece = rounded[:, q * HEAD : (q + 1) * HEAD]
            for z in range(N_Z):
                w_out[z, q, :, kv * HEAD : (kv + 1) * HEAD] = piece


def adam(master, grad, first, second):
    shape = jax.ShapeDtypeStruct(master.shape, F32)
    return pl.pallas_call(
        adam_kernel,
        out_shape=(shape, shape, shape, jax.ShapeDtypeStruct((N_Z, N_GEN, ROWS, 2 * HEAD), BF16)),
        in_specs=[pl.BlockSpec(memory_space=pl.ANY)] * 4,
        out_specs=(whole(),) * 4,
        scratch_shapes=[
            pltpu.VMEM((4,) + master.shape, F32),
            pltpu.SemaphoreType.DMA((4,)),
        ],
        compiler_params=params(VMEM_MOST),
        cost_estimate=SMALL,
        name="adam",
    )(master, grad, first, second)


def columns_kernel(x_ref, _, out_ref, low_ref, high_ref):
    block = x_ref[...].reshape(TOKENS, DEPTH)
    out_ref[0] = block
    low_ref[0] = block[: TOKENS // 2]
    high_ref[0] = block[TOKENS // 2 :]


def columns(inputs, later):
    def shape(rows):
        return jax.ShapeDtypeStruct((N_Y, rows, DEPTH), BF16)

    def block(rows):
        return pl.BlockSpec((1, rows, DEPTH), lambda i: (i, 0, 0))

    return pl.pallas_call(
        columns_kernel,
        grid=(N_Y,),
        in_specs=[
            pl.BlockSpec((ROLL, STEPS, DEPTH), lambda i: (0, 0, i)),
            pl.BlockSpec(memory_space=pl.ANY),
        ],
        out_specs=(block(TOKENS), block(TOKENS // 2), block(TOKENS // 2)),
        out_shape=(shape(TOKENS), shape(TOKENS // 2), shape(TOKENS // 2)),
        compiler_params=params(),
        cost_estimate=SMALL,
        name="columns",
    )(inputs, later)


OLD_BLOCK = 8
PIECE = TOKENS // N_Y
LOG2E = 1.4426950408889634


def old_kernel(prefix, q_ref, k_ref, v_ref, _, out_ref, lse_ref, qp_ref, bias_ref):
    step = pl.program_id(0)
    span = CACHE * HEADS
    block = range(OLD_BLOCK)

    @pl.when(step == 0)
    def _():
        row, col = iota((TOKENS, span), 0), iota((TOKENS, span), 1)
        bias_ref[...] = jnp.where(col % HEADS == row // 32, 0.0, masked_score)

    row, col = iota((TOKENS, TOKENS), 0), iota((TOKENS, TOKENS), 1)
    perm = ((col % 32 == row // 4) & (col // 32 == row % 4)).astype(BF16)
    lane = iota((1, span), 1)
    query = [
        jnp.dot(perm, q_ref[n], preferred_element_type=F32).astype(BF16) for n in block
    ]
    for n in block:
        qp_ref[n] = query[n]
    score = [
        lax.dot_general(
            query[n], k_ref[n], (((1,), (1,)), ((), ())), preferred_element_type=F32
        )
        for n in block
    ]
    score = [
        score[n]
        + bias_ref[...]
        + jnp.where(lane < prefix[step * OLD_BLOCK + n] * HEADS, 0.0, masked_score)
        for n in block
    ]
    top = [jnp.max(s, axis=1, keepdims=True) for s in score]
    weight = [jnp.exp2((s - t) * (SCALE * LOG2E)) for s, t in zip(score, top)]
    total = [jnp.sum(w, axis=1, keepdims=True) for w in weight]
    mixed = [
        jnp.dot(weight[n].astype(BF16), v_ref[n], preferred_element_type=F32) for n in block
    ]
    for n in block:
        out_ref[n] = mixed[n] * (1.0 / total[n])
        lse_ref[n] = jnp.broadcast_to(top[n] * SCALE + jnp.log(total[n]), (TOKENS, HEAD))


def old_attention(prefix, queries, keys, values, later):
    span = CACHE * HEADS
    inside = pl.BlockSpec((OLD_BLOCK, TOKENS, HEAD), lambda i, *_: (i, 0, 0))
    cache = pl.BlockSpec((OLD_BLOCK, span, HEAD), lambda i, *_: (i, 0, 0))
    rows = (ROLL, TOKENS, HEAD)
    return pl.pallas_call(
        old_kernel,
        grid_spec=pltpu.PrefetchScalarGridSpec(
            num_scalar_prefetch=1,
            grid=(ROLL // OLD_BLOCK,),
            in_specs=[inside, cache, cache, pl.BlockSpec(memory_space=pl.ANY)],
            out_specs=(inside, inside, inside),
            scratch_shapes=[pltpu.VMEM((TOKENS, span), F32)],
        ),
        out_shape=(
            jax.ShapeDtypeStruct(rows, F32),
            jax.ShapeDtypeStruct(rows, F32),
            jax.ShapeDtypeStruct(rows, BF16),
        ),
        compiler_params=params(VMEM_MOST),
        cost_estimate=SMALL,
        name="old_attention",
    )(prefix, queries, keys, values, later)


def halves_kernel(before, beyond, _, low, high):
    low[...] = before[...]
    high[...] = beyond[...]


def halves(before, beyond, later):
    half = (DEPTH // 2, 2 * HEAD)
    low, high = pl.BlockSpec(half, lambda i: (0, 0)), pl.BlockSpec(half, lambda i: (1, 0))
    shape = jax.ShapeDtypeStruct(half, BF16)
    return pl.pallas_call(
        halves_kernel,
        grid=(1,),
        in_specs=[low, high, pl.BlockSpec(memory_space=pl.ANY)],
        out_specs=(low, low),
        out_shape=(shape,) * 2,
        compiler_params=params(VMEM_LEAST),
        cost_estimate=SMALL,
        name="halves",
    )(before, beyond, later)


def project_kernel(shifts, sources, carried, last, me, *refs):
    weights, refs = refs[: len(shifts)], refs[len(shifts) :]
    count = 2 if sources == 2 else 6
    own, near, *far = refs[:count]
    out_ref = refs[-1]
    half = TOKENS // 2
    places = [(own, 0, 0, TOKENS), (near, 1, 0, TOKENS)]
    for n, ref in enumerate(far):
        places.append((ref, 2 + n // 2, n % 2 * half, n % 2 * half + half))
    for ref, j, start, stop in places:
        total = refs[count][j, start:stop] if j < carried else None
        at = 0
        for n, (shift, weight) in enumerate(zip(shifts, weights)):
            if n == 0 and j < carried and shift == 0:
                continue
            part = (me[0] + (N_Y - shift)) % N_Y
            depth = weight.shape[0]
            term = jnp.dot(ref[part, :, at : at + depth], weight[...], preferred_element_type=F32)
            total = term if total is None else total + term
            at = (at + depth) % DEPTH
        if last:
            key, value = total[:, :HEAD], total[:, HEAD:]
            high = key.astype(BF16)
            out_ref[j, start:stop, :HEAD] = high
            out_ref[j, start:stop, HEAD : 2 * HEAD] = (key - high.astype(F32)).astype(BF16)
            out_ref[j, start:stop, 2 * HEAD :] = value.astype(BF16)
        else:
            out_ref[j, start:stop] = total


def project(me, shifts, weights, inputs, total, last, *later):
    width, dtype = (3 * HEAD, BF16) if last else (2 * HEAD, F32)
    sources = 2 if len(inputs) == 2 else N_GEN
    carried = () if total is None else (total,)
    return pl.pallas_call(
        functools.partial(
            project_kernel, shifts, sources, 0 if total is None else total.shape[0], last
        ),
        in_specs=[pl.BlockSpec(memory_space=pltpu.SMEM)]
        + [whole()] * (len(weights) + len(inputs) + len(carried))
        + [pl.BlockSpec(memory_space=pl.ANY)] * len(later),
        out_specs=whole(),
        out_shape=jax.ShapeDtypeStruct((sources, TOKENS, width), dtype),
        compiler_params=params(VMEM_LEAST),
        cost_estimate=SMALL,
        name="project",
    )(me, *weights, *inputs, *carried, *later)


FRESH_BLOCK = 16
QUAD = 4


def fresh_kernel(
    dest, slot, lengths, me, p0, p1, p2, p3, cos_ref, sin_ref, qp_ref, lse_ref, old_ref,
    q_one, lse_one, *refs,
):
    kv_ref, out_ref, more_ref = refs[-3:]
    step = ROLL // FRESH_BLOCK - 1 - pl.program_id(0)

    @pl.when(pl.program_id(0) == 0)
    def _():
        cosine, sine = cos_ref[...], sin_ref[...]
        for j, part in enumerate((p0, p1, p2, p3)):
            g = me[1] ^ j
            key = part[:, :HEAD].astype(F32) + part[:, HEAD : 2 * HEAD].astype(F32)
            key = key / jnp.sqrt(jnp.mean(key * key, axis=-1, keepdims=True) + norm_eps)
            key = key * cosine + pltpu.roll(key, HEAD // 2, 1) * sine
            kv_ref[0, g] = key.astype(BF16)
            kv_ref[1, g] = part[:, 2 * HEAD :]
        out_ref[...] = jnp.zeros_like(out_ref)
        more_ref[...] = jnp.zeros_like(more_ref)
        late_rows(me, dest, slot, lengths, q_one, lse_one, kv_ref, out_ref)

    wide = QUAD * STEPS * HEADS
    row, col = iota((QUAD * TOKENS, wide), 0), iota((QUAD * TOKENS, wide), 1)
    own = (
        (row // TOKENS == (col % 16) // STEPS)
        & (row % TOKENS // 32 == col // 16)
        & (col % STEPS <= row % STEPS)
    )
    tall = iota((QUAD * TOKENS, 1), 0)
    groups = range(FRESH_BLOCK // QUAD)
    fresh = [
        [
            jnp.concatenate(
                [
                    kv_ref[
                        kind,
                        g,
                        pl.ds(pl.multiple_of((step * len(groups) + n) * 16, 16), 16),
                    ]
                    for g in range(HEADS)
                ],
                axis=0,
            )
            for n in groups
        ]
        for kind in range(2)
    ]

    def rows(ref, n):
        return ref[n * QUAD : (n + 1) * QUAD].reshape(QUAD * TOKENS, HEAD)

    score = [
        lax.dot_general(
            rows(qp_ref, n), fresh[0][n], (((1,), (1,)), ((), ())), preferred_element_type=F32
        )
        for n in groups
    ]
    score = [jnp.where(own, s * SCALE, masked_score) for s in score]
    lse = [rows(lse_ref, n)[:, :1] for n in groups]
    top = [jnp.maximum(jnp.max(s, axis=1, keepdims=True), old) for s, old in zip(score, lse)]
    weight = [jnp.exp(s - t) for s, t in zip(score, top)]
    share = [jnp.exp(old - t) for old, t in zip(lse, top)]
    total = [jnp.sum(w, axis=1, keepdims=True) + a for w, a in zip(weight, share)]
    for n in reversed(groups):
        first = step * FRESH_BLOCK + n * QUAD
        length = lengths[first]
        for k in range(1, QUAD):
            length = jnp.where(tall < k * TOKENS, length, lengths[first + k])
        kept = (tall % STEPS) < length
        scale = jnp.where(kept, 1.0 / total[n], 0.0)
        mixed = (share[n] * scale) * rows(old_ref, n) + jnp.dot(
            (weight[n] * scale).astype(BF16), fresh[1][n], preferred_element_type=F32
        )
        mixed = mixed.astype(BF16)
        for k in reversed(range(QUAD)):
            d, j = dest[first + k], slot[first + k]
            row = mixed[k * TOKENS : (k + 1) * TOKENS]
            out_ref[d, :TOKENS] = row
            more_ref[jnp.where(j == 1, d, N_FSDP)] = row


def late_rows(me, dest, slot, lengths, q_one, lse_one, kv_ref, out_ref):
    r = me[2]
    start = pl.multiple_of(r // QUAD * 16, 16)
    keys, values = (
        jnp.concatenate([kv_ref[kind, g, pl.ds(start, 16)] for g in range(HEADS)], axis=0)
        for kind in range(2)
    )
    score = lax.dot_general(
        keys, q_one[0], (((1,), (1,)), ((), ())), preferred_element_type=F32
    )
    row, lane = iota((64, TOKENS), 0), iota((64, TOKENS), 1)
    own = (
        (row // 16 == lane // 32)
        & (row % 16 // STEPS == r % QUAD)
        & (row % STEPS <= lane % STEPS)
    )
    score = jnp.where(own, score * SCALE, masked_score)
    eye = iota((TOKENS, TOKENS), 0) == iota((TOKENS, TOKENS), 1)
    old = jnp.sum(jnp.where(eye, lse_one[0], 0.0), axis=0, keepdims=True)
    top = jnp.maximum(jnp.max(score, axis=0, keepdims=True), old)
    weight, share = jnp.exp(score - top), jnp.exp(old - top)
    total = jnp.sum(weight, axis=0, keepdims=True) + share
    kept = (iota((1, TOKENS), 1) % STEPS) < lengths[r]
    scale = jnp.where(kept, 1.0 / total, 0.0)
    weight, share = weight * scale, share * scale
    rows = weight[0:8]
    for n in range(8, 64, 8):
        rows = rows + weight[n : n + 8]
    rows = rows + pltpu.roll(rows, 4, 0)
    place = iota((8, TOKENS), 0)
    rows = jnp.where(place < 4, rows, jnp.where(place == 4, share, 0.0))
    rows = jnp.concatenate([rows, jnp.zeros_like(rows)], axis=0)
    pick = (
        iota((16, 64), 1) == iota((16, 64), 0) // 4 * 16 + r % QUAD * 4 + iota((16, 64), 0) % 4
    ).astype(BF16)
    values = jnp.dot(pick, values, preferred_element_type=F32).astype(BF16)
    seconds = lax.fori_loop(0, ROLL, lambda n, a: a + (slot[n] > 0).astype(jnp.int32), 0)
    count = jnp.where(iota((16, TOKENS), 0) == 5, seconds.astype(F32), 0.0)
    for d in range(N_FSDP):
        out_ref[d, TOKENS + 16 :] = count.astype(BF16)
    d = dest[r]
    out_ref[d, TOKENS : TOKENS + 16] = values
    out_ref[d, TOKENS + 16 :] = (rows + count).astype(BF16)


def fresh(dest, slot, lengths, me, parts, cosine, sine, queries, lse, old):
    def whole_block(shape):
        return pl.BlockSpec(shape, lambda i, *_: (0,) * len(shape))

    steps = ROLL // FRESH_BLOCK
    inside = pl.BlockSpec((FRESH_BLOCK, TOKENS, HEAD), lambda i, *_: (steps - 1 - i, 0, 0))
    one = pl.BlockSpec((1, TOKENS, HEAD), lambda i, dest, slot, lengths, me: (me[2], 0, 0))
    kv = (2, HEADS, TOKENS, HEAD)
    out = (N_FSDP, TOKENS + 32, HEAD)
    more = (N_FSDP + 1, TOKENS, HEAD)
    return pl.pallas_call(
        fresh_kernel,
        grid_spec=pltpu.PrefetchScalarGridSpec(
            num_scalar_prefetch=4,
            grid=(steps,),
            in_specs=[whole_block((TOKENS, 3 * HEAD))] * 4
            + [whole_block((TOKENS, HEAD))] * 2
            + [inside] * 3
            + [one] * 2,
            out_specs=(whole_block(kv), whole_block(out), whole_block(more)),
        ),
        out_shape=tuple(jax.ShapeDtypeStruct(shape, BF16) for shape in (kv, out, more)),
        compiler_params=params(),
        cost_estimate=SMALL,
        name="fresh",
    )(dest, slot, lengths, me, *parts, cosine, sine, queries, lse, old, queries, lse)


def second_kernel(me, old_ref, _, out_ref):
    row = old_ref[0].astype(BF16)
    for z in range(N_Z):
        out_ref[z] = row


def second(me, old, later):
    return pl.pallas_call(
        second_kernel,
        grid_spec=pltpu.PrefetchScalarGridSpec(
            num_scalar_prefetch=1,
            grid=(1,),
            in_specs=[
                pl.BlockSpec((1, TOKENS, HEAD), lambda i, me: (me[2], 0, 0)),
                pl.BlockSpec(memory_space=pl.ANY),
            ],
            out_specs=pl.BlockSpec((N_Z, TOKENS, HEAD), lambda i, me: (0, 0, 0)),
        ),
        out_shape=jax.ShapeDtypeStruct((N_Z, TOKENS, HEAD), BF16),
        compiler_params=params(),
        cost_estimate=SMALL,
        name="second",
    )(me, old, later)


def join_kernel(me, in_ref, e0, e1, e2, e3, _, out_ref, most_ref, seen_ref):
    step = pl.program_id(0)

    @pl.when(step == 0)
    def _():
        seen_ref[...] = jnp.zeros_like(seen_ref)

    eye = iota((TOKENS, TOKENS), 0) == iota((TOKENS, TOKENS), 1)
    row8 = iota((8, 128), 0)
    same = iota((16, 128), 1) // 32 == iota((16, 128), 0) // 4
    block = range(N_Z)

    def body(extra):
        for n in block:
            out_ref[n, 0] = in_ref[n, :TOKENS]
        tiles = [in_ref[n, TOKENS + 16 :, :].astype(F32)[:8] for n in block]
        most = tiles[0]
        for tile in tiles[1:]:
            most = jnp.maximum(most, tile)
        seen_ref[...] = jnp.maximum(seen_ref[...], most)
        diags = [jnp.where(eye, tile[4:5], 0.0).astype(BF16) for tile in tiles]
        both = [jnp.where(row8 < 4, tile, pltpu.roll(tile, 4, 0)) for tile in tiles]
        weights = [
            jnp.where(same, jnp.concatenate([w, w], axis=0), 0.0).astype(BF16) for w in both
        ]
        kept = [
            jnp.dot(diags[n], extra[n], preferred_element_type=F32) for n in block
        ]
        added = [
            lax.dot_general(
                weights[n],
                in_ref[n, TOKENS : TOKENS + 16, :],
                (((0,), (0,)), ((), ())),
                preferred_element_type=F32,
            )
            for n in block
        ]
        for n in block:
            out_ref[n, 1] = (kept[n] + added[n]).astype(BF16)

    for k, extra in enumerate((e0, e1, e2, e3)):
        pl.when(step == k)(functools.partial(body, extra))

    @pl.when(step == pl.num_programs(0) - 1)
    def _():
        most_ref[0] = jnp.max(seen_ref[5:6, :]).astype(jnp.int32)


def join(me, rows, extras, later):
    def of_source(i, me):
        return (me[0] + N_Y - i) % N_Y

    return pl.pallas_call(
        join_kernel,
        grid_spec=pltpu.PrefetchScalarGridSpec(
            num_scalar_prefetch=1,
            grid=(N_Y,),
            in_specs=[pl.BlockSpec((N_Z, TOKENS + 32, HEAD), lambda i, me: (of_source(i, me), 0, 0))]
            + [pl.BlockSpec((N_Z, TOKENS, HEAD), lambda i, me: (0, 0, 0))] * 4
            + [pl.BlockSpec(memory_space=pl.ANY)],
            out_specs=(
                pl.BlockSpec(
                    (N_Z, SLOTS, TOKENS, HEAD), lambda i, me: (of_source(i, me), 0, 0, 0)
                ),
                pl.BlockSpec(memory_space=pltpu.SMEM),
            ),
            scratch_shapes=[pltpu.VMEM((8, HEAD), F32)],
        ),
        out_shape=(
            jax.ShapeDtypeStruct((N_FSDP, SLOTS, TOKENS, HEAD), BF16),
            jax.ShapeDtypeStruct((1,), jnp.int32),
        ),
        compiler_params=params(),
        cost_estimate=SMALL,
        name="join",
    )(me, rows, *extras, later)


def in_rows(joined):
    joined = joined.reshape(N_FSDP, SLOTS, 8 * HEADS, STEPS, HEAD).transpose(0, 1, 3, 2, 4)
    return joined.reshape(1, 1, N_FSDP, SLOTS, STEPS, 8 * HEADS * HEAD)


def turn_tables(prefix_lengths):
    half_size = HEAD // 2
    exponent = -2.0 * jnp.arange(half_size).astype(F32) / HEAD
    inverse_freq = jnp.power(jnp.float32(rope_theta), exponent)
    positions = prefix_lengths[:, None] + jnp.arange(STEPS, dtype=jnp.int32)[None, :]
    angle = positions.reshape(TOKENS, 1).astype(F32) * inverse_freq
    cosine, sine = jnp.cos(angle), jnp.sin(angle)
    return (
        jnp.concatenate([cosine, cosine], axis=-1),
        jnp.concatenate([-sine, sine], axis=-1),
    )


def along(moves):
    def place_of(x):
        return (x % 2) * 2 + x // 2

    return [(place_of(start), place_of(stop)) for start, stop in moves]


def shift_y(k):
    return [(y, (y + k) % N_Y) for y in range(N_Y)]


def on_device(
    master_weight,
    gradient,
    first_moment,
    second_moment,
    new_inputs,
    queries,
    cache_keys,
    cache_values,
    prefix_lengths,
    rollout_lengths,
    destinations,
):
    new_master, new_first, new_second, blocks = adam(
        master_weight, gradient, first_moment, second_moment
    )
    own_rows = lax.all_to_all(
        blocks.reshape(N_Z * N_GEN, ROWS, 2 * HEAD), ("z", "xl", "c"), 0, 0, tiled=True
    ).reshape(DEPTH, 2 * HEAD)

    core = [(0, 1), (1, 0)]
    own, low, high = columns(new_inputs, blocks)
    right = [(x, (x + 1) % 4) for x in range(4)]
    left = [(x, (x + 3) % 4) for x in range(4)]
    near = lax.ppermute(own, "c", core)
    far_a = lax.ppermute(low, ("xl", "tp"), along(right))
    far_b = lax.ppermute(high, ("xl", "tp"), along(left))
    both_a, both_b = (lax.ppermute(far, "c", core) for far in (far_a, far_b))
    inputs = (own, near, far_a, far_b, both_a, both_b)

    same_dest = destinations[:, None] == destinations[None, :]
    earlier = jnp.arange(ROLL)[None, :] < jnp.arange(ROLL)[:, None]
    slot_rank = jnp.sum((same_dest & earlier).astype(jnp.int32), axis=1)
    old_rows, lse, ordered = old_attention(
        prefix_lengths,
        queries.reshape(ROLL, TOKENS, HEAD),
        cache_keys.reshape(ROLL, CACHE * HEADS, HEAD),
        cache_values.reshape(ROLL, CACHE * HEADS, HEAD),
        own,
    )
    own_rows = after(own_rows, lse)
    one = jnp.argmax(slot_rank).astype(jnp.int32)
    me = jnp.stack([lax.axis_index("y"), lax.axis_index("xl") * 2 + lax.axis_index("c"), one])
    before = lax.ppermute(own_rows, "y", shift_y(1))
    beyond = lax.ppermute(own_rows, "y", shift_y(-1))
    total = project(me, (0,), (own_rows,), inputs[:2], None, False)
    extra = lax.all_to_all(second(me, old_rows, total), "z", 0, 0, tiled=True)
    low, high = halves(before, beyond, total)
    across = [lax.ppermute(low, "y", shift_y(1)), lax.ppermute(high, "y", shift_y(-1))]
    total = project(me, (0, 1, 3), (own_rows, before, beyond), inputs, total, False)
    parts = project(me, (2, 2), across, inputs, total, True, extra)
    parts = [parts[0]] + [
        lax.ppermute(parts[j], ("xl", "c"), [(q, q ^ j) for q in range(N_GEN)]) for j in (1, 2, 3)
    ]
    cosine, sine = turn_tables(prefix_lengths)
    fresh_parts, rows, more = fresh(
        destinations, slot_rank, rollout_lengths, me, parts, cosine, sine, ordered, lse, old_rows
    )
    rows = lax.all_to_all(rows, ("y", "z"), 0, 0, tiled=True)
    extras = [extra] + [lax.ppermute(extra, "y", shift_y(k)) for k in (1, 2, 3)]
    fresh_kv = fresh_parts.reshape(2, HEADS, ROLL, STEPS, HEAD).transpose(2, 3, 0, 1, 4)
    joined, most = join(me, rows, extras, fresh_kv)

    def with_all_seconds():
        seconds = lax.all_to_all(more[:N_FSDP], ("y", "z"), 0, 0, tiled=True)
        return jnp.stack([joined[:, 0], seconds], axis=1)

    returned_rows = in_rows(after(lax.cond(most[0] > 1, with_all_seconds, lambda: joined)))
    return (new_master, new_first, new_second, fresh_kv, returned_rows)


def solution(mesh):
    fine = Mesh(mesh.devices.reshape(N_Y, N_Z, 2, 2, 2), ("y", "z", "xl", "c", "tp"))
    group = ("y", "z", "xl", "c")
    rows = P(None, group, "tp")
    in_specs = (
        rows,
        rows,
        rows,
        rows,
        P(group, None, None),
        P(group, None, "tp", None),
        P(group, None, "tp", None),
        P(group, None, "tp", None),
        P(group),
        P(group),
        P(group),
    )
    out_specs = (
        rows,
        rows,
        rows,
        P(group, None, None, "tp", None),
        P(("y", "z"), ("xl", "c"), None, None, None, "tp"),
    )
    return jax.shard_map(
        on_device, mesh=fine, in_specs=in_specs, out_specs=out_specs, check_vma=False
    )
```
